128 devices in a mesh: rotor: 8 (over y, core), tower: 16 (over z, x).
Axes of the slice: x: 4, y: 4, z: 4, core: 2. Of those that a mesh axis runs over, the one named last changes fastest.
Arguments:
- solution: float32 [2, 5, 2, 16, 64, 4096], P(None, None, None, 'rotor', None, 'tower'), may hold values from -0.5 to 2.8, as said below
- fringe_owner: int32 [8, 16, 2, 128, 1], P('rotor', 'tower'), may hold values from 0 to 127; in each aligned block of 128 rows (0 to 127, 128 to 255, ..., all dimensions but the last counted through in order) at most 2 rows name the same one
- fringe_donor: int32 [8, 16, 2, 128], P('rotor', 'tower'), may hold values from 0 to 1023, as said below
- fringe_target: int32 [8, 16, 2, 128], P('rotor', 'tower'), may hold values from 0 to 65535, as said below
- fringe_weight: float32 [8, 16, 2, 128, 64], P('rotor', 'tower'), may hold values from 0.01171875 to 0.01953125
Outputs:
- advanced: float32 [2, 5, 2, 16, 64, 4096], P(None, None, None, 'rotor', None, 'tower')
The draws below stay inside these ranges and needn't reach their ends.
Inputs may be any that keep to these rules, and one draw needn't show every extreme that they name: `fringe_owner`: in the fringe list of one device for one section at most 2 points have the same owner, and some owner has exactly 2. `fringe_donor`: the donor's grid differs from the grid of the point's target. `fringe_target`: the targets of one device's list for one section are distinct. `solution`: in field 0 density and pressure lie in 0.9 to 1.1 and each velocity component in -0.15 to 0.15; field 1 lies in -0.5 to 0.6.
All inputs are finite; a program needn't handle non-finite values.
Results may differ from the reference program's by a relative error of at most 0.0003.
Values sent between devices are 32-bit elements; how exact they have to be, the bound alone decides.
No kernel may reach another device: no remote copies, remote signals or barrier semaphores. Data moves between devices by JAX's collectives and lax.ppermute only.
A program may use at most 256 MiB of HBM per device.

```python
import math
from functools import partial
import jax
import jax.numpy as jnp
import numpy as np
from jax import lax

NPTS = 64
VARS = 5
SECTIONS = 2
EX = 2
EY = 2
EZ = 128
FRINGE = 128
CAP = 2
N_ROTOR = 8
N_TOWER = 16


def draw_solution(key, part):
    grid_shape = (2, NPTS, EX * N_ROTOR, EY * N_TOWER, EZ)
    keys_list = [jax.random.fold_in(key, 31 + offset) for offset in range(10)]
    density = 1.0 + 0.1 * jax.random.uniform(keys_list[0], grid_shape, jnp.float32, -1.0, 1.0)
    velocities = [0.15 * jax.random.uniform(keys_list[1 + component], grid_shape, jnp.float32, -1.0, 1.0) for component in range(3)]
    pressure = 1.0 + 0.1 * jax.random.uniform(keys_list[4], grid_shape, jnp.float32, -1.0, 1.0)
    tangent = 0.5 * jax.random.uniform(keys_list[5], (5,) + grid_shape, jnp.float32, -1.0, 1.0)
    kinetic = 0.5 * density * (velocities[0] * velocities[0] + velocities[1] * velocities[1] + velocities[2] * velocities[2])
    primal = jnp.stack([density, density * velocities[0], density * velocities[1], density * velocities[2], pressure / 0.4 + kinetic])
    whole = jnp.stack([primal, tangent]).astype(jnp.float32)
    whole = whole.reshape(2, 5, 2, NPTS, EX * N_ROTOR, EY * N_TOWER * EZ)
    return jnp.transpose(whole, (0, 1, 2, 4, 3, 5))


def fringe_pair(key):
    element_count = EX * EY * EZ
    list_shape = (N_ROTOR, N_TOWER, SECTIONS, FRINGE)
    stride = 2 * NPTS * element_count // FRINGE
    chosen = jax.random.randint(jax.random.fold_in(key, 71), list_shape, 0, stride, dtype=jnp.int32)
    rows_at = jnp.arange(FRINGE, dtype=jnp.int32)
    chosen = jnp.where(rows_at == 0, 0, chosen)
    chosen = jnp.where(rows_at == FRINGE - 1, stride - 1, chosen)
    target_id = rows_at * stride + chosen
    grid_of = target_id // (NPTS * element_count)
    element = jax.random.randint(jax.random.fold_in(key, 72), list_shape, 0, element_count, dtype=jnp.int32)
    donor_id = (1 - grid_of) * element_count + element
    return (donor_id.astype(jnp.int32), target_id.astype(jnp.int32))


def draw_fringe_donor(key, part):
    return fringe_pair(key)[0]


def draw_fringe_target(key, part):
    return fringe_pair(key)[1]


def block_scale(own_key, extent, shards, low, high):
    factor_of = 1.0
    for position, blocks in shards:
        draws = jax.random.uniform(jax.random.fold_in(jax.random.fold_in(own_key, 6), position), (blocks,), jnp.float32, low / len(shards), high / len(shards))
        factor_of = factor_of * jnp.repeat(jnp.exp(draws), extent[position] // blocks).reshape((-1,) + (1,) * (len(extent) - 1 - position))
    return factor_of


def shared_out(own_key, own, number, rows, number_of, top, limit, skew):
    ranking = jax.random.permutation(own_key, number_of)
    crowded, ordinary = portions_of(number_of, rows * top, limit, skew, True), portions_of(number_of, rows * top, limit, skew, False)
    places = jnp.arange(number_of)

    def named(tallies, offset_by):
        used = int((tallies > 0).sum())
        fixed = max(1, used // 4)
        passed = fixed + (places - fixed + offset_by * (used - fixed)) % max(1, number_of - fixed)
        return jnp.zeros((number_of,), jnp.int32).at[ranking[jnp.where(places < fixed, places, passed)]].set(jnp.asarray(tallies, jnp.int32))

    tallies = jnp.where(number % 4 == 0, named(crowded, number // 4), named(ordinary, number - number // 4 - 1))
    mixed = jax.random.permutation(jax.random.fold_in(own, 3), number_of)
    donor, sink = mixed[0:number_of // 2 * 2:2], mixed[1:number_of // 2 * 2:2]
    room = jnp.minimum(tallies[donor] - 1, limit - tallies[sink]) // 2
    room = jnp.where((donor == ranking[0]) | (sink == ranking[0]) | (tallies[sink] == 0), 0, jnp.maximum(room, 0))
    passed = jax.random.randint(jax.random.fold_in(own, 4), (number_of // 2,), 0, 1 << 20) % (room + 1)
    tallies = tallies.at[donor].add(-passed).at[sink].add(passed)
    items = jnp.searchsorted(jnp.cumsum(tallies), jnp.arange(rows * top), side="right").astype(jnp.int32)
    table = items.reshape(top, rows).T
    table = table[jax.random.permutation(jax.random.fold_in(own, 1), rows)]
    offset_by = jax.random.randint(jax.random.fold_in(own, 2), (rows, 1), 0, top)
    return jnp.take_along_axis(table, (jnp.arange(top)[None, :] + offset_by) % top, axis=1)


def portions_of(count, total, reach, slope, full):
    loads = [(1 << 20) // math.isqrt(standing ** slope) + 1 for standing in range(1, count + 1)]
    largest = reach if full else min(reach, max(-(-total // count), total * loads[0] // sum(loads)))
    least = 1 if total - largest >= count - 1 else 0
    holding, surplus = [largest] + [least] * (count - 1), total - largest - least * (count - 1)
    while surplus > 0:
        candidates = [i for i in range(1, count) if holding[i] < largest] or [i for i in range(1, count) if holding[i] < reach]
        pool, remaining = sum([loads[i] for i in candidates]), surplus
        for i in candidates:
            extra = min(reach - holding[i], max(1, remaining * loads[i] // pool), surplus)
            holding[i] = holding[i] + extra
            surplus = surplus - extra
    return np.array(holding)


def setup_inputs(seed: int = 0) -> dict:
    key_list = jax.random.split(jax.random.key(seed), 6)
    solution = draw_solution(jax.random.fold_in(key_list[5], 71), 0)
    fringe_owner_keys = jax.random.split(jax.random.fold_in(key_list[1], 1), N_ROTOR * N_TOWER * SECTIONS * FRINGE // FRINGE)
    fringe_owner_turns = jax.random.permutation(jax.random.fold_in(key_list[1], 3), N_ROTOR * N_TOWER * SECTIONS * FRINGE // FRINGE)
    fringe_owner = jax.vmap(lambda own, number: shared_out(jax.random.fold_in(key_list[1], 2), own, number, FRINGE, N_ROTOR * N_TOWER, 1, CAP, 2))(fringe_owner_keys, fringe_owner_turns).reshape((N_ROTOR, N_TOWER, SECTIONS, FRINGE, 1))
    fringe_donor = draw_fringe_donor(jax.random.fold_in(key_list[5], 71), 0)
    fringe_target = draw_fringe_target(jax.random.fold_in(key_list[5], 71), 0)
    fringe_weight = jnp.clip(0.01171875 + 0.0078125 * jax.random.uniform(key_list[4], (N_ROTOR, N_TOWER, SECTIONS, FRINGE, NPTS), jnp.float32) ** block_scale(key_list[4], (N_ROTOR, N_TOWER, SECTIONS, FRINGE, NPTS), ((0, 8), (1, 16)), -0.2, 0.2), 0.01171875, 0.01953125)
    return dict(solution=solution, fringe_owner=fringe_owner, fringe_donor=fringe_donor, fringe_target=fringe_target, fringe_weight=fringe_weight)


gamma_less = 0.4
gamma_full = 1.4
time_step = 0.01
highest = lax.Precision.HIGHEST

def lagrange_values(nodes_at, location):
    values = np.ones(len(nodes_at))
    for column in range(len(nodes_at)):
        for other_node in range(len(nodes_at)):
            if other_node != column:
                values[column] *= (location - nodes_at[other_node]) / (nodes_at[column] - nodes_at[other_node])
    return values

def lagrange_slopes(nodes_at, location):
    node_count = len(nodes_at)
    slopes = np.zeros(node_count)
    for column in range(node_count):
        for skipped in range(node_count):
            if skipped != column:
                factor = 1.0 / (nodes_at[column] - nodes_at[skipped])
                for other_node in range(node_count):
                    if other_node != column and other_node != skipped:
                        factor *= (location - nodes_at[other_node]) / (nodes_at[column] - nodes_at[other_node])
                slopes[column] += factor
    return slopes

def expand_table(factor_block, axis_id):
    identity = np.eye(4)
    pieces = [identity, identity, identity]
    pieces[axis_id] = factor_block
    return np.kron(np.kron(pieces[0], pieces[1]), pieces[2])

def build_tables():
    gauss_nodes = np.array([-0.8611363115940526, -0.3399810435848563, 0.3399810435848563, 0.8611363115940526])
    gauss_weights = np.array([0.3478548451374538, 0.6521451548625461, 0.6521451548625461, 0.3478548451374538])
    slope_rows = np.stack([lagrange_slopes(gauss_nodes, location) for location in gauss_nodes])
    low_end = lagrange_values(gauss_nodes, -1.0)
    high_end = lagrange_values(gauss_nodes, 1.0)
    diffs = np.stack([expand_table(slope_rows, axis_id) for axis_id in range(3)])
    lows = np.stack([expand_table(low_end[None, :], axis_id) for axis_id in range(3)])
    highs = np.stack([expand_table(high_end[None, :], axis_id) for axis_id in range(3)])
    lift_lows = np.stack([expand_table((low_end / gauss_weights)[:, None], axis_id) for axis_id in range(3)])
    lift_highs = np.stack([expand_table((high_end / gauss_weights)[:, None], axis_id) for axis_id in range(3)])
    return tuple((np.asarray(one_table, dtype=np.float32) for one_table in (diffs, lows, highs, lift_lows, lift_highs)))

def apply_table(matrix, values):
    return jnp.einsum('pq,fvgqxyz->fvgpxyz', jnp.asarray(matrix), values, precision=highest)

def thermo(state_vars):
    density = state_vars[0]
    momenta = [state_vars[1], state_vars[2], state_vars[3]]
    energy = state_vars[4]
    kinetic = 0.5 * (momenta[0] * momenta[0] + momenta[1] * momenta[1] + momenta[2] * momenta[2]) / density
    pressure = gamma_less * (energy - kinetic)
    return (density, momenta, energy, pressure)

def euler_flux(state_vars, direction):
    density, momenta, energy, pressure = thermo(state_vars)
    velocity = momenta[direction] / density
    rows_out = [momenta[direction]]
    for component in range(3):
        addend = momenta[component] * velocity
        if component == direction:
            addend = addend + pressure
        rows_out.append(addend)
    rows_out.append((energy + pressure) * velocity)
    return jnp.stack(rows_out)

def wave_speed(state_vars, direction):
    density, momenta, energy, pressure = thermo(state_vars)
    velocity = momenta[direction] / density
    sound_sq = gamma_full * pressure / density
    return jnp.sqrt(sound_sq) + jnp.sqrt(velocity * velocity + sound_sq)

def rusanov(left_state, right_state, direction):
    spread = 0.25 * (wave_speed(left_state, direction) + wave_speed(right_state, direction))
    average = 0.5 * (euler_flux(left_state, direction) + euler_flux(right_state, direction))
    return average - spread * (right_state - left_state)

def face_terms(tables, fluxes, low_trace, high_trace, outer_low, outer_high, direction):
    diff_tables, low_tables, high_tables, lift_low_tables, lift_high_tables = tables
    axis_pos = 4 + direction
    extent_along = low_trace.shape[axis_pos]
    left_states = jnp.concatenate([outer_low, high_trace], axis=axis_pos)
    right_states = jnp.concatenate([low_trace, outer_high], axis=axis_pos)
    common_p, common_t = jax.jvp(partial(rusanov, direction=direction), (left_states[0], right_states[0]), (left_states[1], right_states[1]))
    common = jnp.stack([common_p, common_t])
    common_low = lax.slice_in_dim(common, 0, extent_along, axis=axis_pos)
    common_high = lax.slice_in_dim(common, 1, extent_along + 1, axis=axis_pos)
    high_part = apply_table(lift_high_tables[direction], common_high - apply_table(high_tables[direction], fluxes))
    low_part = apply_table(lift_low_tables[direction], common_low - apply_table(low_tables[direction], fluxes))
    return high_part - low_part

def residual(field_now):
    tables = build_tables()
    diff_tables, low_tables, high_tables = (tables[0], tables[1], tables[2])
    primal, tangent = (field_now[0], field_now[1])
    summed = jnp.zeros_like(field_now)
    for direction in range(3):
        fluxes = jnp.stack(jax.jvp(partial(euler_flux, direction=direction), (primal,), (tangent,)))
        low_trace = apply_table(low_tables[direction], field_now)
        high_trace = apply_table(high_tables[direction], field_now)
        axis_pos = 4 + direction
        extent_along = field_now.shape[axis_pos]
        outer_low = lax.slice_in_dim(low_trace, 0, 1, axis=axis_pos)
        outer_high = lax.slice_in_dim(high_trace, extent_along - 1, extent_along, axis=axis_pos)
        summed = summed + apply_table(diff_tables[direction], fluxes) + face_terms(tables, fluxes, low_trace, high_trace, outer_low, outer_high, direction)
    return summed

def with_fringe(field_now, section_id, fringe_owner, fringe_donor, fringe_target, fringe_weight):
    element_count = EX * EY * EZ
    owner_flat = fringe_owner[:, :, section_id, :, 0].reshape(-1)
    donor_flat = fringe_donor[:, :, section_id].reshape(-1)
    target_flat = fringe_target[:, :, section_id].reshape(-1)
    weight_flat = fringe_weight[:, :, section_id].reshape(-1, NPTS)
    owner_row = owner_flat // N_TOWER
    owner_col = owner_flat % N_TOWER
    donor_grid = donor_flat // element_count
    donor_elem = donor_flat % element_count
    picked = field_now[:, :, donor_grid, :, owner_row * EX + donor_elem // (EY * EZ), owner_col * EY + donor_elem // EZ % EY, donor_elem % EZ]
    own_values = lax.optimization_barrier(jnp.sum(picked * weight_flat[:, None, None, :], axis=-1))
    list_shape = (N_ROTOR, N_TOWER, fringe_target.shape[3])
    row_ids = jnp.broadcast_to(jnp.arange(N_ROTOR, dtype=jnp.int32)[:, None, None], list_shape).reshape(-1)
    col_ids = jnp.broadcast_to(jnp.arange(N_TOWER, dtype=jnp.int32)[None, :, None], list_shape).reshape(-1)
    target_grid = target_flat // (NPTS * element_count)
    target_point = target_flat // element_count % NPTS
    target_elem = target_flat % element_count
    return field_now.at[:, :, target_grid, target_point, row_ids * EX + target_elem // (EY * EZ), col_ids * EY + target_elem // EZ % EY, target_elem % EZ].set(jnp.moveaxis(own_values, 0, -1))

def reference(solution, fringe_owner, fringe_donor, fringe_target, fringe_weight):
    grid_x = solution.shape[3]
    grid_y = solution.shape[5] // EZ
    inner = jnp.transpose(solution, (0, 1, 2, 4, 3, 5)).reshape(2, VARS, 2, NPTS, grid_x, grid_y, EZ)
    first_field = with_fringe(inner, 0, fringe_owner, fringe_donor, fringe_target, fringe_weight)
    middle = first_field - time_step * residual(first_field)
    second = with_fringe(middle, 1, fringe_owner, fringe_donor, fringe_target, fringe_weight)
    result = 0.5 * first_field + 0.5 * (second - time_step * residual(second))
    return jnp.transpose(result.reshape(2, VARS, 2, NPTS, grid_x, grid_y * EZ), (0, 1, 2, 4, 3, 5))
```

```python
from functools import partial

import jax
import jax.numpy as jnp
import numpy as np
from jax import lax
from jax.experimental import pallas as pl
from jax.experimental.pallas import tpu as pltpu
from jax.sharding import PartitionSpec as P

DT = 0.01
DEV = 128
AXES = ("rotor", "tower")
F32, BF16, I32 = jnp.float32, jnp.bfloat16, jnp.int32
HIGH = lax.Precision.HIGHEST


def lagrange_values(nodes, at):
    values = np.ones(4)
    for j in range(4):
        for m in range(4):
            if m != j:
                values[j] *= (at - nodes[m]) / (nodes[j] - nodes[m])
    return values


def lagrange_slopes(nodes, at):
    slopes = np.zeros(4)
    for j in range(4):
        for k in range(4):
            if k != j:
                factor = 1.0 / (nodes[j] - nodes[k])
                for m in range(4):
                    if m != j and m != k:
                        factor *= (at - nodes[m]) / (nodes[j] - nodes[m])
                slopes[j] += factor
    return slopes


def expand(block, axis):
    pieces = [np.eye(4)] * 3
    pieces[axis] = block
    return np.kron(np.kron(pieces[0], pieces[1]), pieces[2])


NODES = np.array([-0.8611363115940526, -0.3399810435848563, 0.3399810435848563, 0.8611363115940526])
QUAD = np.array([0.3478548451374538, 0.6521451548625461, 0.6521451548625461, 0.3478548451374538])
SLOPES = np.stack([lagrange_slopes(NODES, at) for at in NODES])
LOW, HIGHV = lagrange_values(NODES, -1.0), lagrange_values(NODES, 1.0)
LIFT_LO, LIFT_HI = LOW / QUAD, HIGHV / QUAD


def halves(table):
    hi = table.astype(np.float32).astype(jnp.bfloat16)
    lo = (table - hi.astype(np.float64)).astype(jnp.bfloat16)
    return hi, lo


def tables():
    e_lo = [expand(LOW[None, :], d) for d in range(3)]
    e_hi = [expand(HIGHV[None, :], d) for d in range(3)]
    l_lo = [expand(LIFT_LO[:, None], d) for d in range(3)]
    l_hi = [expand(LIFT_HI[:, None], d) for d in range(3)]
    weak = [expand(SLOPES, d) - l_hi[d] @ e_hi[d] + l_lo[d] @ e_lo[d] for d in range(3)]
    main = np.concatenate(weak + [-l_lo[1], l_hi[1], -l_lo[2], l_hi[2]], axis=1)
    trace = np.concatenate([t for d in range(3) for t in (e_lo[d], e_hi[d])], axis=0)
    t_hi, t_lo = halves(trace)
    return main, np.concatenate([t_hi, t_hi, t_lo], axis=1)


MAIN, TRACE = tables()


def iota(shape, dim):
    return lax.broadcasted_iota(I32, shape, dim)


def dot(a, b, precision=None):
    return lax.dot_general(a, b, (((1,), (0,)), ((), ())), precision=precision, preferred_element_type=F32)


def split(x):
    hi = x.astype(BF16)
    return hi, (x - hi.astype(F32)).astype(BF16)


def pick4(index, values):
    out = jnp.full(index.shape, float(values[3]), F32)
    for i in range(3):
        out = jnp.where(index == i, float(values[i]), out)
    return out


def primitive(u):
    rho, m1, m2, m3, en = u
    r = 1.0 / rho
    v = [m1 * r, m2 * r, m3 * r]
    vv = v[0] * v[0] + v[1] * v[1] + v[2] * v[2]
    p = 0.4 * (en - 0.5 * rho * vv)
    return r, v, vv, p


def tangent(du, r, v, vv):
    dv = [(du[1 + i] - v[i] * du[0]) * r for i in range(3)]
    dp = 0.4 * (du[4] - (v[0] * du[1] + v[1] * du[2] + v[2] * du[3]) + 0.5 * vv * du[0])
    return dv, dp


def flux(u, du, v, p, dv, dp, d):
    out = [u[1 + d]]
    dout = [du[1 + d]]
    for i in range(3):
        f = u[1 + i] * v[d]
        df = du[1 + i] * v[d] + u[1 + i] * dv[d]
        if i == d:
            f, df = f + (p - 1.0), df + dp
        out.append(f)
        dout.append(df)
    out.append((u[4] + p) * v[d])
    dout.append((du[4] + dp) * v[d] + (u[4] + p) * dv[d])
    return out, dout


def side(w, d):
    u, du = w[:5], w[5:]
    r, v, vv, p = primitive(u)
    dv, dp = tangent(du, r, v, vv)
    f, df = flux(u, du, v, p, dv, dp, d)
    c2 = 1.4 * p * r
    dc2 = 1.4 * r * dp - c2 * r * du[0]
    s2 = v[d] * v[d] + c2
    r1, r2 = lax.rsqrt(c2), lax.rsqrt(s2)
    s = c2 * r1 + s2 * r2
    ds = 0.5 * dc2 * r1 + (v[d] * dv[d] + 0.5 * dc2) * r2
    return f + df, s, ds


def common(left, right, d):
    fl, sl, dsl = side(left, d)
    fr, sr, dsr = side(right, d)
    s, ds = 0.25 * (sl + sr), 0.25 * (dsl + dsr)
    out = []
    for i in range(5):
        out.append(0.5 * (fl[i] + fr[i]) - s * (right[i] - left[i]))
    for i in range(5):
        out.append(
            0.5 * (fl[5 + i] + fr[5 + i]) - ds * (right[i] - left[i]) - s * (right[5 + i] - left[5 + i])
        )
    return out, fl, fr


def request_kernel(owner, donor, target, weight, req, trow, tcol):
    sub, lane = iota((DEV, DEV), 0), iota((DEV, DEV), 1)
    results = []
    tc = [jnp.zeros((DEV, DEV), F32) for _ in range(2)]
    for sec in range(2):
        oc = jnp.broadcast_to(owner[0, 0, sec].astype(F32), (DEV, DEV))
        orow = oc.T
        same = (oc == orow) & (sub < lane)
        pos = jnp.sum(jnp.where(same, 1.0, 0.0), axis=0, keepdims=True)
        dc = jnp.broadcast_to(donor[0, 0, sec : sec + 1].astype(F32), (DEV, DEV)).T
        tg = jnp.broadcast_to(target[0, 0, sec : sec + 1].astype(F32) + 1.0, (DEV, DEV)).T
        w = jnp.concatenate([weight[0, 0, sec], jnp.zeros((DEV, 64), F32)], axis=1)
        rhs = jnp.where(lane == 64, dc, jnp.where(lane == 65, tg, w))
        for s in range(2):
            chosen = (orow == sub.astype(F32)) & (pos == float(s))
            res = dot(jnp.where(chosen, 1.0, 0.0), rhs, HIGH)
            results.append(res)
            tc[s] = jnp.where(lane == sec, res[:, 65:66], tc[s])
    for sec in range(2):
        pair = jnp.where(lane < 64, results[2 * sec], pltpu.roll(results[2 * sec + 1], 64, 1))
        req[:, sec * 128 : sec * 128 + 128] = pair
    ids = jnp.zeros((DEV, DEV), F32)
    for i in range(4):
        ids = jnp.where(lane == i, results[i][:, 64:65], ids)
    req[:, 256:384] = ids
    for s in range(2):
        tcol[s * 128 : s * 128 + 128, :] = tc[s]
        trow[:, s * 128 : s * 128 + 128] = tc[s].T[0:8]


def point_row(trow, sec):
    return (trow[sec : sec + 1, :].astype(I32) - 1) >> 9


def element_col(tcol, sec, count):
    return jnp.broadcast_to((tcol[:, sec : sec + 1].astype(I32) - 1) & 511, (256, count))


def target_mask(trow, tcol, sec, g):
    at = jnp.where(iota((64, 256), 0) + 64 * g == point_row(trow, sec), 1.0, 0.0).astype(BF16)
    where = jnp.where(iota((256, 512), 1) == element_col(tcol, sec, 512), 1.0, 0.0).astype(BF16)
    return dot(at, where)


def outer_traces(get, mask, trace_table, outs):
    xlo, xhi, ylo, yhi = outs
    keep = [mask[:, x * 256 : x * 256 + 256] < 0.5 for x in range(2)]
    e2 = trace_table[32:64, :]
    for c in range(10):
        w = [jnp.where(keep[x], get(c, x), 0.0) for x in range(2)]
        xlo[0, c] = sum(float(LOW[a]) * w[0][16 * a : 16 * a + 16] for a in range(4))
        xhi[0, c] = sum(float(HIGHV[a]) * w[1][16 * a : 16 * a + 16] for a in range(4))
        for y, out in ((0, ylo), (1, yhi)):
            both = jnp.concatenate([w[x][:, y * 128 : y * 128 + 128] for x in range(2)], axis=1)
            hi, lo = split(both)
            res = dot(e2[16 * y : 16 * y + 16], jnp.concatenate([hi, lo, hi], axis=0))
            out[0, c] = res


def trace_kernel(field, trow, tcol, table, *outs):
    g = pl.program_id(0)
    mask = target_mask(trow, tcol, 0, g)
    outer_traces(lambda c, x: field[c // 5, c % 5, 0, x], mask, table, outs)
    info = jnp.concatenate([trow[0:2, :], jnp.ones((1, 256), F32), jnp.zeros((13, 256), F32)], axis=0)
    for out in outs:
        out[0, 10] = info


def interpolate_part(field_rows, asked, sec, base, picks, first):
    ids = asked[256 + 2 * sec : 256 + 2 * sec + 2, :]
    row = jnp.concatenate([ids[0:1], ids[1:2]], axis=1).astype(I32)
    chosen = jnp.where(iota((256, 256), 0) + base == row, 1.0, 0.0).astype(BF16)
    hi, lo = split(field_rows)
    part = dot(hi, chosen) + dot(lo, chosen)

    @pl.when(first)
    def _():
        picks[...] = part

    @pl.when(jnp.logical_not(first))
    def _():
        picks[...] += part


def answer(asked, sec, picks):
    w = jnp.concatenate([asked[sec * 128 : sec * 128 + 64], asked[sec * 128 + 64 : sec * 128 + 128]], axis=1)
    rows = [jnp.sum(picks[64 * c : 64 * c + 64, :] * w, axis=0, keepdims=True) for c in range(10)]
    value = jnp.concatenate(
        [r[:, 0:128] for r in rows]
        + [jnp.zeros((2, 128), F32)]
        + [r[:, 128:256] for r in rows]
        + [jnp.zeros((2, 128), F32)],
        axis=0,
    )
    groups = [value] + [pltpu.roll(value, by, 1) for by in (16, 112, 1, 127)] + [jnp.zeros((8, 128), F32)]
    return jnp.concatenate(groups, axis=0).T


def interpolate_kernel(field, req, resp, asked, picks):
    g = pl.program_id(0)

    @pl.when(g == 0)
    def _():
        asked[...] = req[...].T

    for x in range(2):
        rows = jnp.concatenate([field[c // 5, c % 5, 0, x] for c in range(10)], axis=0)
        first = (g == 0) if x == 0 else jnp.bool_(False)
        interpolate_part(rows, asked, 0, g * 512 + x * 256, picks, first)

    @pl.when(g == 1)
    def _():
        resp[...] = answer(asked, 0, picks)


def section_kernel(last, *refs):
    it = iter(refs)
    take = lambda n: [next(it) for _ in range(n)]
    (field,) = take(1)
    (first_in,) = take(1) if last else (None,)
    (req,) = take(1) if not last else (None,)
    resp, trow, tcol, main_t, trace_t = take(5)
    halo = take(4)
    info = take(4)
    if last:
        (result,) = take(1)
        (now,) = take(1)
    else:
        now_ref, result, resp_out = take(3)
        halo_out = take(4)
        (now,) = take(1)
    (got, lhs, xl, xr, yl, yr, zl, zr, hx, hy, hz, vol) = take(12)
    if not last:
        asked, picks = take(2)
    g = pl.program_id(0)
    sec = 1 if last else 0

    @pl.when(g == 0)
    def _():
        got[...] = resp[...].T
        if not last:
            asked[...] = req[...].T

    def values(j):
        both = got[24 * j : 24 * j + 24, :]
        return jnp.concatenate([both[0:10], both[12:22]], axis=1)

    val = values(0)
    at = iota((64, 256), 0) + 64 * g == point_row(trow, sec)
    for c in range(10):
        hi, lo = split(jnp.where(at, val[c : c + 1], 0.0))
        lhs[64 * c : 64 * c + 64, 0:256] = hi
        lhs[64 * c : 64 * c + 64, 256:512] = lo
    where = jnp.where(iota((256, 512), 1) == element_col(tcol, sec, 512), 1.0, 0.0).astype(BF16)
    mask = dot(jnp.where(at, 1.0, 0.0).astype(BF16), where)
    for x in range(2):
        wx = where[:, x * 256 : x * 256 + 256]
        scat = dot(lhs[...], jnp.concatenate([wx, wx], axis=0))
        hit = mask[:, x * 256 : x * 256 + 256] > 0.5
        for c in range(10):
            now[c, x] = jnp.where(hit, scat[64 * c : 64 * c + 64], field[c // 5, c % 5, 0, x])

    for c in range(10):
        for x in range(2):
            hi, lo = split(now[c, x])
            res = dot(trace_t[...], jnp.concatenate([hi, lo, hi], axis=0))
            xr[c, x] = res[0:16]
            xl[c, x + 1] = res[16:32]
            yr[c, x, 0] = res[32:48, 0:128]
            yr[c, x, 1] = res[32:48, 128:256]
            yl[c, x, 1] = res[48:64, 0:128]
            yl[c, x, 2] = res[48:64, 128:256]
            zr[c, x] = res[64:80]
            zl[c, x] = res[80:96]

    for j in range(4):
        row2 = info[j][0, 0, sec : sec + 1, :]
        present = info[j][0, 0, 2:3, 0:128] > 0.5
        pt = (row2.astype(I32) - 1) >> 9
        q = pt & 63
        elem = (row2.astype(I32) - 1) & 511
        weights = HIGHV if j % 2 == 0 else LOW
        if j < 2:
            fp, coef = q & 15, pick4(q >> 4, weights)
            want = 1 if j == 0 else 0
            place = jnp.where((elem >> 8) == want, elem & 255, -1)
        else:
            fp, coef = ((q >> 4) << 2) | (q & 3), pick4((q >> 2) & 3, weights)
            want = 1 if j == 2 else 0
            place = jnp.where(((elem >> 7) & 1) == want, ((elem >> 8) << 7) | (elem & 127), -1)
        coef = jnp.where((pt >> 6) == g, coef, 0.0)
        nval = values(1 + j) * coef
        hit = iota((16, 256), 0) == fp
        his, los = [], []
        for c in range(10):
            hi, lo = split(jnp.where(hit, nval[c : c + 1], 0.0))
            his.append(hi)
            los.append(lo)
        left = jnp.concatenate([jnp.concatenate(his, axis=0), jnp.concatenate(los, axis=0)], axis=1)
        pcol = jnp.broadcast_to(place.astype(F32), (128, 256)).T
        pcol = jnp.concatenate([pcol, pcol], axis=1)
        there = jnp.where(iota((256, 256), 1).astype(F32) == pcol, 1.0, 0.0).astype(BF16)
        fix = dot(left, jnp.concatenate([there, there], axis=0))
        for c in range(10):
            for t in range(2):
                lanes = slice(128 * t, 128 * t + 128)
                theirs = halo[j][0, c, :, lanes] + fix[16 * c : 16 * c + 16, lanes]
                if j == 0:
                    xl[c, 0, :, lanes] = jnp.where(present, theirs, xr[c, 0, :, lanes])
                elif j == 1:
                    xr[c, 2, :, lanes] = jnp.where(present, theirs, xl[c, 2, :, lanes])
                elif j == 2:
                    yl[c, t, 0] = jnp.where(present, theirs, yr[c, t, 0])
                else:
                    yr[c, t, 2] = jnp.where(present, theirs, yl[c, t, 2])

    for t in range(2):
        lanes = slice(128 * t, 128 * t + 128)

        @pl.loop(0, 3)
        def _(face):
            left = [xl[c, face, :, lanes] for c in range(10)]
            right = [xr[c, face, :, lanes] for c in range(10)]
            out, _, _ = common(left, right, 0)
            for c in range(10):
                hx[c, face, :, lanes] = out[c]

    @pl.loop(0, 6)
    def _(i):
        x, face = i // 3, i % 3
        left = [yl[c, x, face] for c in range(10)]
        right = [yr[c, x, face] for c in range(10)]
        out, _, _ = common(left, right, 1)
        for c in range(10):
            hy[c, x, face] = out[c].astype(BF16)

    edge = iota((16, 128), 1) == 0
    for t in range(2):
        lanes = slice(128 * t, 128 * t + 128)

        @pl.loop(0, 2)
        def _(x):
            left = [pltpu.roll(zl[c, x, :, lanes], 1, 1) for c in range(10)]
            right = [zr[c, x, :, lanes] for c in range(10)]
            out, fl, fr = common(left, right, 2)
            for c in range(10):
                hz[c, x, 0:16, lanes] = jnp.where(edge, fr[c], out[c]).astype(BF16)
                hz[c, x, 16:32, lanes] = pltpu.roll(jnp.where(edge, fl[c], out[c]), 127, 1).astype(BF16)

    @pl.loop(0, 8)
    def _(i):
        x, q = i // 4, pl.multiple_of((i % 4) * 16, 16)
        for t in range(2):
            lanes = slice(128 * t, 128 * t + 128)
            w = [now[c, x, pl.ds(q, 16), lanes] for c in range(10)]
            u, du = w[:5], w[5:]
            r, v, vv, p = primitive(u)
            dv, dp = tangent(du, r, v, vv)
            for d in range(3):
                f, df = flux(u, du, v, p, dv, dp, d)
                for c in range(10):
                    vol[c, x, pl.ds(64 * d + q, 16), lanes] = (f + df)[c].astype(BF16)

    scale = DT * 0.5 if last else DT
    for c in range(10):
        for x in range(2):
            faces = [hy[c, x, i] for i in range(3)]
            stacked = jnp.concatenate(
                [
                    vol[c, x],
                    jnp.concatenate([faces[0], faces[1]], axis=1),
                    jnp.concatenate([faces[1], faces[2]], axis=1),
                    hz[c, x],
                ],
                axis=0,
            )
            res = dot(main_t[...], stacked)
            low, high = hx[c, x], hx[c, x + 1]
            for a in range(4):
                rows = slice(16 * a, 16 * a + 16)
                lift = float(-scale * LIFT_HI[a]) * high + float(scale * LIFT_LO[a]) * low
                mine = now[c, x, rows]
                if last:
                    base = 0.5 * (mine + first_in[c // 5, c % 5, 0, x, rows])
                else:
                    base = mine
                    now_ref[c // 5, c % 5, 0, x, rows] = mine
                result[c // 5, c % 5, 0, x, rows] = base + (res[rows] + lift)

    if not last:
        for x in range(2):
            rows = jnp.concatenate([result[c // 5, c % 5, 0, x] for c in range(10)], axis=0)
            start = (g == 0) if x == 0 else jnp.bool_(False)
            interpolate_part(rows, asked, 1, g * 512 + x * 256, picks, start)
        outer_traces(
            lambda c, x: result[c // 5, c % 5, 0, x], target_mask(trow, tcol, 1, g), trace_t, halo_out
        )

        @pl.when(g == 1)
        def _():
            resp_out[...] = answer(asked, 1, picks)


FIELD = (2, 5, 2, 2, 64, 256)


def field_spec():
    return pl.BlockSpec((2, 5, 1, 2, 64, 256), lambda g: (0, 0, g, 0, 0, 0))


def whole(shape):
    return pl.BlockSpec(shape, lambda g: (0,) * len(shape))


def halo_spec(comps):
    return pl.BlockSpec((1, comps, 16, 256), lambda g: (g, 0, 0, 0))


def shape(*dims):
    return jax.ShapeDtypeStruct(dims, F32)


def params(mb):
    return pltpu.CompilerParams(dimension_semantics=("arbitrary",), vmem_limit_bytes=mb * 2**20)


def shift(x, axis, up):
    n = lax.axis_size(axis)
    pairs = [(i, i + 1) if up else (i + 1, i) for i in range(n - 1)]
    return lax.ppermute(x, axis, pairs)


def to_neighbours(traces):
    xlo, xhi, ylo, yhi = traces
    return [
        shift(xhi, "rotor", True),
        shift(xlo, "rotor", False),
        shift(yhi, "tower", True),
        shift(ylo, "tower", False),
    ]


def exchange(x):
    return lax.all_to_all(x, AXES, split_axis=0, concat_axis=0, tiled=True)


def section_call(last, scale, field, first, req, resp, trow, tcol, halos, infos):
    main_t = jnp.asarray((scale * MAIN).astype(np.float32), BF16)
    operands = [field] + ([first] if last else [req]) + [resp, trow, tcol, main_t, jnp.asarray(TRACE)]
    specs = [field_spec()] + ([field_spec()] if last else [whole((128, 384))])
    specs += [whole((128, 128)), whole((8, 256)), whole((256, 128)), whole((64, 256)), whole((96, 192))]
    operands += list(halos) + list(infos)
    specs += [halo_spec(10)] * 4 + [pl.BlockSpec((1, 1, 16, 256), lambda g: (0, 10, 0, 0))] * 4
    scratch = [
        pltpu.VMEM((10, 2, 64, 256), F32),
        pltpu.VMEM((128, 128), F32),
        pltpu.VMEM((640, 512), BF16),
        pltpu.VMEM((10, 3, 16, 256), F32),
        pltpu.VMEM((10, 3, 16, 256), F32),
        pltpu.VMEM((10, 2, 3, 16, 128), F32),
        pltpu.VMEM((10, 2, 3, 16, 128), F32),
        pltpu.VMEM((10, 2, 16, 256), F32),
        pltpu.VMEM((10, 2, 16, 256), F32),
        pltpu.VMEM((10, 3, 16, 256), F32),
        pltpu.VMEM((10, 2, 3, 16, 128), BF16),
        pltpu.VMEM((10, 2, 32, 256), BF16),
        pltpu.VMEM((10, 2, 192, 256), BF16),
    ]
    if last:
        out_shape, out_specs = shape(*FIELD), field_spec()
    else:
        out_shape = [shape(*FIELD), shape(*FIELD), shape(128, 128)] + [shape(2, 10, 16, 256)] * 4
        out_specs = [field_spec(), field_spec(), whole((128, 128))] + [halo_spec(10)] * 4
        scratch += [pltpu.VMEM((384, 128), F32), pltpu.VMEM((640, 256), F32)]
    return pl.pallas_call(
        partial(section_kernel, last),
        grid=(2,),
        in_specs=specs,
        out_specs=out_specs,
        out_shape=out_shape,
        scratch_shapes=scratch,
        compiler_params=params(48),
        cost_estimate=pl.CostEstimate(flops=2 * 10**9, bytes_accessed=10**7, transcendentals=0),
        name="section_last" if last else "section_first",
    )(*operands)


def on_device(field, owner, donor, target, weight):
    req, trow, tcol = pl.pallas_call(
        request_kernel,
        out_shape=[shape(128, 384), shape(8, 256), shape(256, 128)],
        compiler_params=pltpu.CompilerParams(vmem_limit_bytes=16 * 2**20),
        name="request",
    )(owner, donor, target, weight)
    req = exchange(req)
    traces = pl.pallas_call(
        trace_kernel,
        grid=(2,),
        in_specs=[field_spec(), whole((8, 256)), whole((256, 128)), whole((96, 192))],
        out_specs=[halo_spec(11)] * 4,
        out_shape=[shape(2, 11, 16, 256)] * 4,
        compiler_params=params(24),
        cost_estimate=pl.CostEstimate(flops=10**8, bytes_accessed=4 * 10**6, transcendentals=0),
        name="traces",
    )(field, trow, tcol, jnp.asarray(TRACE))
    infos = to_neighbours(traces)
    resp = pl.pallas_call(
        interpolate_kernel,
        grid=(2,),
        in_specs=[field_spec(), whole((128, 384))],
        out_specs=whole((128, 128)),
        out_shape=shape(128, 128),
        scratch_shapes=[pltpu.VMEM((384, 128), F32), pltpu.VMEM((640, 256), F32)],
        compiler_params=params(24),
        cost_estimate=pl.CostEstimate(flops=10**9, bytes_accessed=4 * 10**6, transcendentals=0),
        name="interpolate",
    )(field, req)
    resp = exchange(resp)
    first, middle, resp, *traces = section_call(
        False, -DT, field, None, req, resp, trow, tcol, infos, infos
    )
    halos = to_neighbours(traces)
    resp = exchange(resp)
    return section_call(True, -0.5 * DT, middle, first, None, resp, trow, tcol, halos, infos)


def solution(mesh):
    placed = (
        P(None, None, None, "rotor", None, "tower"),
        P("rotor", "tower", None, None, None),
        P("rotor", "tower", None, None),
        P("rotor", "tower", None, None),
        P("rotor", "tower", None, None, None),
    )
    return jax.shard_map(
        on_device,
        mesh=mesh,
        in_specs=placed,
        out_specs=P(None, None, None, "rotor", None, "tower"),
        check_vma=False,
    )
```

```python
from functools import partial

import jax
import jax.numpy as jnp
import numpy as np
from jax import lax
from jax.experimental import pallas as pl
from jax.experimental.pallas import tpu as pltpu
from jax.sharding import PartitionSpec as P

DT = 0.01
DEV = 128
AXES = ("rotor", "tower")
F32, BF16, I32 = jnp.float32, jnp.bfloat16, jnp.int32
HIGH = lax.Precision.HIGHEST


def lagrange_values(nodes, at):
    values = np.ones(4)
    for j in range(4):
        for m in range(4):
            if m != j:
                values[j] *= (at - nodes[m]) / (nodes[j] - nodes[m])
    return values


def lagrange_slopes(nodes, at):
    slopes = np.zeros(4)
    for j in range(4):
        for k in range(4):
            if k != j:
                factor = 1.0 / (nodes[j] - nodes[k])
                for m in range(4):
                    if m != j and m != k:
                        factor *= (at - nodes[m]) / (nodes[j] - nodes[m])
                slopes[j] += factor
    return slopes


def expand(block, axis):
    pieces = [np.eye(4)] * 3
    pieces[axis] = block
    return np.kron(np.kron(pieces[0], pieces[1]), pieces[2])


NODES = np.array([-0.8611363115940526, -0.3399810435848563, 0.3399810435848563, 0.8611363115940526])
QUAD = np.array([0.3478548451374538, 0.6521451548625461, 0.6521451548625461, 0.3478548451374538])
SLOPES = np.stack([lagrange_slopes(NODES, at) for at in NODES])
LOW, HIGHV = lagrange_values(NODES, -1.0), lagrange_values(NODES, 1.0)
LIFT_LO, LIFT_HI = LOW / QUAD, HIGHV / QUAD


def halves(table):
    hi = table.astype(np.float32).astype(jnp.bfloat16)
    lo = (table - hi.astype(np.float64)).astype(jnp.bfloat16)
    return hi, lo


def tables():
    e_lo = [expand(LOW[None, :], d) for d in range(3)]
    e_hi = [expand(HIGHV[None, :], d) for d in range(3)]
    l_lo = [expand(LIFT_LO[:, None], d) for d in range(3)]
    l_hi = [expand(LIFT_HI[:, None], d) for d in range(3)]
    weak = [expand(SLOPES, d) - l_hi[d] @ e_hi[d] + l_lo[d] @ e_lo[d] for d in range(3)]
    main = np.concatenate(weak + [-l_lo[2], l_hi[2], -l_lo[1], l_hi[1]], axis=1)
    trace = np.concatenate([t for d in range(3) for t in (e_lo[d], e_hi[d])], axis=0)
    t_hi, t_lo = halves(trace)
    return main, np.concatenate([t_hi, t_hi, t_lo], axis=1)


MAIN, TRACE = tables()


def iota(shape, dim):
    return lax.broadcasted_iota(I32, shape, dim)


def dot(a, b, precision=None):
    return lax.dot_general(a, b, (((1,), (0,)), ((), ())), precision=precision, preferred_element_type=F32)


def split(x):
    hi = x.astype(BF16)
    return hi, (x - hi.astype(F32)).astype(BF16)


def pick4(index, values):
    out = jnp.full(index.shape, float(values[3]), F32)
    for i in range(3):
        out = jnp.where(index == i, float(values[i]), out)
    return out


def primitive(u):
    rho, m1, m2, m3, en = u
    r = 1.0 / rho
    v = [m1 * r, m2 * r, m3 * r]
    vv = v[0] * v[0] + v[1] * v[1] + v[2] * v[2]
    p = 0.4 * (en - 0.5 * rho * vv)
    return r, v, vv, p


def tangent(du, r, v, vv):
    dv = [(du[1 + i] - v[i] * du[0]) * r for i in range(3)]
    dp = 0.4 * (du[4] - (v[0] * du[1] + v[1] * du[2] + v[2] * du[3]) + 0.5 * vv * du[0])
    return dv, dp


def flux(u, du, v, p, dv, dp, d):
    out = [u[1 + d]]
    dout = [du[1 + d]]
    for i in range(3):
        f = u[1 + i] * v[d]
        df = du[1 + i] * v[d] + u[1 + i] * dv[d]
        if i == d:
            f, df = f + (p - 1.0), df + dp
        out.append(f)
        dout.append(df)
    out.append((u[4] + p) * v[d])
    dout.append((du[4] + dp) * v[d] + (u[4] + p) * dv[d])
    return out, dout


def side(w, d):
    u, du = w[:5], w[5:]
    r, v, vv, p = primitive(u)
    dv, dp = tangent(du, r, v, vv)
    f, df = flux(u, du, v, p, dv, dp, d)
    c2 = 1.4 * p * r
    dc2 = 1.4 * r * dp - c2 * r * du[0]
    s2 = v[d] * v[d] + c2
    r1, r2 = lax.rsqrt(c2), lax.rsqrt(s2)
    s = c2 * r1 + s2 * r2
    ds = 0.5 * dc2 * r1 + (v[d] * dv[d] + 0.5 * dc2) * r2
    return f + df, s, ds


def common(left, right, d):
    fl, sl, dsl = side(left, d)
    fr, sr, dsr = side(right, d)
    s, ds = 0.25 * (sl + sr), 0.25 * (dsl + dsr)
    out = []
    for i in range(5):
        out.append(0.5 * (fl[i] + fr[i]) - s * (right[i] - left[i]))
    for i in range(5):
        out.append(
            0.5 * (fl[5 + i] + fr[5 + i]) - ds * (right[i] - left[i]) - s * (right[5 + i] - left[5 + i])
        )
    return out, fl, fr


def request_kernel(owner, donor, target, weight, req, trow, tcol):
    sub, lane = iota((DEV, DEV), 0), iota((DEV, DEV), 1)
    results = []
    tc = [jnp.zeros((DEV, DEV), F32) for _ in range(2)]
    for sec in range(2):
        orow = jnp.broadcast_to(owner[sec : sec + 1].astype(F32), (DEV, DEV))
        oc = orow.T
        same = (oc == orow) & (sub < lane)
        pos = jnp.sum(jnp.where(same, 1.0, 0.0), axis=0, keepdims=True)
        lists = [weight[sec], donor[sec : sec + 1].astype(F32), target[sec : sec + 1].astype(F32) + 1.0]
        rhs = jnp.concatenate(lists + [jnp.zeros((62, DEV), F32)], axis=0).T
        for s in range(2):
            chosen = (orow == sub.astype(F32)) & (pos == float(s))
            res = dot(jnp.where(chosen, 1.0, 0.0), rhs, HIGH)
            results.append(res)
            tc[s] = jnp.where(lane == sec, res[:, 65:66], tc[s])
    for sec in range(2):
        pair = jnp.where(lane < 64, results[2 * sec], pltpu.roll(results[2 * sec + 1], 64, 1))
        req[pl.ds(sec, DEV, stride=3), :] = pair
    ids = jnp.zeros((DEV, DEV), F32)
    for i in range(4):
        ids = jnp.where(lane == i, results[i][:, 64:65], ids)
    req[pl.ds(2, DEV, stride=3), :] = ids
    for s in range(2):
        tcol[s * 128 : s * 128 + 128, :] = tc[s]
        trow[:, s * 128 : s * 128 + 128] = tc[s].T[0:8]


def point_row(trow, sec):
    return (trow[sec : sec + 1, :].astype(I32) - 1) >> 9


def element_col(tcol, sec, count):
    return jnp.broadcast_to((tcol[:, sec : sec + 1].astype(I32) - 1) & 511, (256, count))


def target_mask(trow, tcol, sec, g):
    at = jnp.where(iota((64, 256), 0) + 64 * g == point_row(trow, sec), 1.0, 0.0).astype(BF16)
    where = jnp.where(iota((256, 512), 1) == element_col(tcol, sec, 512), 1.0, 0.0).astype(BF16)
    return dot(at, where)


def outer_traces(get, mask, trace_table, outs):
    xlo, xhi, ylo, yhi = outs
    keep = [mask[:, x * 256 : x * 256 + 256] < 0.5 for x in range(2)]
    e2 = trace_table[32:64, :]
    for c in range(10):
        w = [jnp.where(keep[x], get(c, x), 0.0) for x in range(2)]
        xlo[0, c] = sum(float(LOW[a]) * w[0][16 * a : 16 * a + 16] for a in range(4))
        xhi[0, c] = sum(float(HIGHV[a]) * w[1][16 * a : 16 * a + 16] for a in range(4))
        for y, out in ((0, ylo), (1, yhi)):
            both = jnp.concatenate([w[x][:, y * 128 : y * 128 + 128] for x in range(2)], axis=1)
            hi, lo = split(both)
            res = dot(e2[16 * y : 16 * y + 16], jnp.concatenate([hi, lo, hi], axis=0))
            out[0, c] = res


def trace_kernel(sec, field, trow, tcol, table, *outs):
    g = pl.program_id(0)
    mask = target_mask(trow, tcol, sec, g)
    outer_traces(lambda c, x: field[c // 5, c % 5, 0, x], mask, table, outs)
    if sec == 1:
        return
    info = jnp.concatenate([trow[0:2, :], jnp.ones((1, 256), F32), jnp.zeros((13, 256), F32)], axis=0)
    for out in outs:
        out[0, 10] = info


def load_asked(req, asked):
    for i in range(3):
        asked[i * 128 : i * 128 + 128, :] = req[pl.ds(i, DEV, stride=3), :].T


def interpolate_part(field_rows, asked, sec, base, picks, first):
    ids = asked[256 + 2 * sec : 256 + 2 * sec + 2, :]
    row = jnp.concatenate([ids[0:1], ids[1:2]], axis=1).astype(I32)
    chosen = jnp.where(iota((256, 256), 0) + base == row, 1.0, 0.0).astype(BF16)
    part = dot(field_rows.astype(BF16), chosen)

    @pl.when(first)
    def _():
        picks[...] = part

    @pl.when(jnp.logical_not(first))
    def _():
        picks[...] += part


def answer(asked, sec, picks):
    w = jnp.concatenate([asked[sec * 128 : sec * 128 + 64], asked[sec * 128 + 64 : sec * 128 + 128]], axis=1)
    rows = [jnp.sum(picks[64 * c : 64 * c + 64, :] * w, axis=0, keepdims=True) for c in range(10)]
    value = jnp.concatenate(
        [r[:, 0:128] for r in rows]
        + [jnp.zeros((2, 128), F32)]
        + [r[:, 128:256] for r in rows]
        + [jnp.zeros((2, 128), F32)],
        axis=0,
    )
    groups = [value] + [pltpu.roll(value, by, 1) for by in (16, 112, 1, 127)] + [jnp.zeros((8, 128), F32)]
    return jnp.concatenate(groups, axis=0).T


def interpolate_kernel(field, req, resp, asked, picks):
    i = pl.program_id(0)

    @pl.when(i == 0)
    def _():
        load_asked(req, asked)

    rows = jnp.concatenate([field[c // 5, c % 5, 0, 0] for c in range(10)], axis=0)
    interpolate_part(rows, asked, 0, i * 256, picks, i == 0)

    @pl.when(i == 3)
    def _():
        resp[...] = answer(asked, 0, picks)


def values(got, j):
    both = got[24 * j : 24 * j + 24, :]
    return jnp.concatenate([both[0:10], both[12:22]], axis=1)


def set_fringe(field, got, trow, tcol, sec, g, lhs, now):
    val = values(got, 0)
    at = iota((64, 256), 0) + 64 * g == point_row(trow, sec)
    for c in range(10):
        hi, lo = split(jnp.where(at, val[c : c + 1], 0.0))
        lhs[64 * c : 64 * c + 64, 0:256] = hi
        lhs[64 * c : 64 * c + 64, 256:512] = lo
    where = jnp.where(iota((256, 512), 1) == element_col(tcol, sec, 512), 1.0, 0.0).astype(BF16)
    mask = dot(jnp.where(at, 1.0, 0.0).astype(BF16), where)
    for x in range(2):
        wx = where[:, x * 256 : x * 256 + 256]
        scat = dot(lhs[...], jnp.concatenate([wx, wx], axis=0))
        hit = mask[:, x * 256 : x * 256 + 256] > 0.5
        for c in range(10):
            now[c, x] = jnp.where(hit, scat[64 * c : 64 * c + 64], field[c // 5, c % 5, 0, x])


def all_traces(now, table, xt, yt, zt):
    for c in range(10):
        for x in range(2):
            hi, lo = split(now[c, x])
            res = dot(table[...], jnp.concatenate([hi, lo, hi], axis=0))
            xt[c, x] = res[0:32]
            yt[c, x] = res[32:64]
            zt[c, x] = res[64:96]


def mend_halos(halo, info, got, sec, g, xt, yt, hal):
    for j in range(4):
        row2 = info[j][0, 0, sec : sec + 1, :]
        present = info[j][0, 0, 2:3, 0:128] > 0.5
        pt = (row2.astype(I32) - 1) >> 9
        q = pt & 63
        elem = (row2.astype(I32) - 1) & 511
        weights = HIGHV if j % 2 == 0 else LOW
        if j < 2:
            fp, coef = q & 15, pick4(q >> 4, weights)
            want = 1 if j == 0 else 0
            place = jnp.where((elem >> 8) == want, elem & 255, -1)
        else:
            fp, coef = ((q >> 4) << 2) | (q & 3), pick4((q >> 2) & 3, weights)
            want = 1 if j == 2 else 0
            place = jnp.where(((elem >> 7) & 1) == want, ((elem >> 8) << 7) | (elem & 127), -1)
        coef = jnp.where((pt >> 6) == g, coef, 0.0)
        nval = values(got, 1 + j) * coef
        hit = iota((16, 256), 0) == fp
        his, los = [], []
        for c in range(10):
            hi, lo = split(jnp.where(hit, nval[c : c + 1], 0.0))
            his.append(hi)
            los.append(lo)
        left = jnp.concatenate([jnp.concatenate(his, axis=0), jnp.concatenate(los, axis=0)], axis=1)
        pcol = jnp.broadcast_to(place.astype(F32), (128, 256)).T
        pcol = jnp.concatenate([pcol, pcol], axis=1)
        there = jnp.where(iota((256, 256), 1).astype(F32) == pcol, 1.0, 0.0).astype(BF16)
        fix = dot(left, jnp.concatenate([there, there], axis=0))
        own = slice(0, 16) if j % 2 == 0 else slice(16, 32)
        for c in range(10):
            for t in range(2):
                lanes = slice(128 * t, 128 * t + 128)
                theirs = halo[j][0, c, :, lanes] + fix[16 * c : 16 * c + 16, lanes]
                if j < 2:
                    mine = xt[c, j, own, lanes]
                else:
                    y = j - 2
                    mine = yt[c, t, own, 128 * y : 128 * y + 128]
                hal[j, c, :, lanes] = jnp.where(present, theirs, mine)


def faces_xy(xt, yt, hal, hx, hy):
    for face in range(3):
        for t in range(2):
            lanes = slice(128 * t, 128 * t + 128)
            left = [hal[0, c, :, lanes] if face == 0 else xt[c, face - 1, 16:32, lanes] for c in range(10)]
            right = [hal[1, c, :, lanes] if face == 2 else xt[c, face, 0:16, lanes] for c in range(10)]
            out, _, _ = common(left, right, 0)
            for c in range(10):
                hx[c, face, :, lanes] = out[c]
    for face in range(3):
        for x in range(2):
            mine = slice(128 * x, 128 * x + 128)
            before = slice(128 * face - 128, 128 * face)
            after = slice(128 * face, 128 * face + 128)
            left = [hal[2, c, :, mine] if face == 0 else yt[c, x, 16:32, before] for c in range(10)]
            right = [hal[3, c, :, mine] if face == 2 else yt[c, x, 0:16, after] for c in range(10)]
            out, _, _ = common(left, right, 1)
            for c in range(10):
                h = out[c].astype(BF16)
                if face < 2:
                    hy[c, x, 0:16, after] = h
                if face > 0:
                    hy[c, x, 16:32, before] = h


def faces_z(zt, hz):
    edge = iota((16, 128), 1) == 0
    for t in range(2):
        lanes = slice(128 * t, 128 * t + 128)
        for x in range(2):
            left = [pltpu.roll(zt[c, x, 16:32, lanes], 1, 1) for c in range(10)]
            right = [zt[c, x, 0:16, lanes] for c in range(10)]
            out, fl, fr = common(left, right, 2)
            for c in range(10):
                hz[c, x, 0:16, lanes] = jnp.where(edge, fr[c], out[c]).astype(BF16)
                hz[c, x, 16:32, lanes] = pltpu.roll(jnp.where(edge, fl[c], out[c]), 127, 1).astype(BF16)


def point_fluxes(now, vol):
    @pl.loop(0, 8, unroll=2)
    def _(i):
        x, q = i // 4, pl.multiple_of((i % 4) * 16, 16)
        for t in range(2):
            lanes = slice(128 * t, 128 * t + 128)
            w = [now[c, x, pl.ds(q, 16), lanes] for c in range(10)]
            u, du = w[:5], w[5:]
            r, v, vv, p = primitive(u)
            dv, dp = tangent(du, r, v, vv)
            for d in range(3):
                f, df = flux(u, du, v, p, dv, dp, d)
                for c in range(10):
                    vol[c, x, pl.ds(64 * d + q, 16), lanes] = (f + df)[c].astype(BF16)


def lift_x(hx, c, x, a, scale):
    return float(-scale * LIFT_HI[a]) * hx[c, x + 1] + float(scale * LIFT_LO[a]) * hx[c, x]


def first_section_kernel(field, req, resp, trow, tcol, main_t, trace_t, *refs):
    halo, info, (now_ref, result, resp_out), scratch = refs[0:4], refs[4:8], refs[8:11], refs[11:]
    now, got, lhs, xt, yt, zt, hal, hx, hy, hz, vol, asked, picks = scratch
    g = pl.program_id(0)

    @pl.when(g == 0)
    def _():
        got[...] = resp[...].T
        load_asked(req, asked)

    set_fringe(field, got, trow, tcol, 0, g, lhs, now)
    all_traces(now, trace_t, xt, yt, zt)
    mend_halos(halo, info, got, 0, g, xt, yt, hal)
    faces_xy(xt, yt, hal, hx, hy)
    faces_z(zt, hz)
    point_fluxes(now, vol)
    for x in range(2):
        for c in range(10):
            res = dot(main_t[...], jnp.concatenate([vol[c, x], hz[c, x], hy[c, x]], axis=0))
            for a in range(4):
                rows = slice(16 * a, 16 * a + 16)
                mine = now[c, x, rows]
                now_ref[c // 5, c % 5, 0, x, rows] = mine
                result[c // 5, c % 5, 0, x, rows] = mine + (res[rows] + lift_x(hx, c, x, a, DT))
    for x in range(2):
        rows = jnp.concatenate([result[c // 5, c % 5, 0, x] for c in range(10)], axis=0)
        start = (g == 0) if x == 0 else jnp.bool_(False)
        interpolate_part(rows, asked, 1, g * 512 + x * 256, picks, start)

    @pl.when(g == 1)
    def _():
        resp_out[...] = answer(asked, 1, picks)


def inner_kernel(field, first, resp, trow, tcol, main_t, trace_t, partial_out, xt_out, yt_out, *scratch):
    now, got, lhs, zt, hz, vol = scratch
    g = pl.program_id(0)

    @pl.when(g == 0)
    def _():
        got[...] = resp[...].T

    set_fringe(field, got, trow, tcol, 1, g, lhs, now)
    all_traces(now, trace_t, xt_out.at[0], yt_out.at[0], zt)
    faces_z(zt, hz)
    point_fluxes(now, vol)
    for x in range(2):
        for c in range(10):
            res = dot(main_t[...], jnp.concatenate([vol[c, x], hz[c, x]], axis=0))
            partial_out[c // 5, c % 5, 0, x] = 0.5 * (now[c, x] + first[c // 5, c % 5, 0, x]) + res


def outer_kernel(part, xt, yt, resp, lift_y, *refs):
    halo, info, result, (got, hal, hx, hy) = refs[0:4], refs[4:8], refs[8], refs[9:]
    g = pl.program_id(0)

    @pl.when(g == 0)
    def _():
        got[...] = resp[...].T

    mend_halos(halo, info, got, 1, g, xt.at[0], yt.at[0], hal)
    faces_xy(xt.at[0], yt.at[0], hal, hx, hy)
    for x in range(2):
        for c in range(10):
            res = dot(lift_y[...], hy[c, x])
            for a in range(4):
                rows = slice(16 * a, 16 * a + 16)
                add = res[rows] + lift_x(hx, c, x, a, 0.5 * DT)
                result[c // 5, c % 5, 0, x, rows] = part[c // 5, c % 5, 0, x, rows] + add


FIELD = (2, 5, 2, 2, 64, 256)


def field_spec():
    return pl.BlockSpec((2, 5, 1, 2, 64, 256), lambda g: (0, 0, g, 0, 0, 0))


def whole(shape):
    return pl.BlockSpec(shape, lambda g: (0,) * len(shape))


def halo_spec(comps):
    return pl.BlockSpec((1, comps, 16, 256), lambda g: (g, 0, 0, 0))


def shape(*dims):
    return jax.ShapeDtypeStruct(dims, F32)


def params(mb):
    return pltpu.CompilerParams(dimension_semantics=("arbitrary",), vmem_limit_bytes=mb * 2**20)


def shift(x, axis, up):
    n = lax.axis_size(axis)
    pairs = [(i, i + 1) if up else (i + 1, i) for i in range(n - 1)]
    return lax.ppermute(x, axis, pairs)


def to_neighbours(traces):
    xlo, xhi, ylo, yhi = traces
    return [
        shift(xhi, "rotor", True),
        shift(xlo, "rotor", False),
        shift(yhi, "tower", True),
        shift(ylo, "tower", False),
    ]


def exchange(x):
    return lax.all_to_all(x, AXES, split_axis=0, concat_axis=0, tiled=True)


def estimate(us):
    return pl.CostEstimate(flops=int(us * 10**9), bytes_accessed=10**5, transcendentals=0)


def vmem(*dims, dtype=F32):
    return pltpu.VMEM(dims, dtype)


def far(x):
    return pltpu.with_memory_space_constraint(x, pltpu.HBM)


def info_specs():
    return [pl.BlockSpec((1, 1, 16, 256), lambda g: (0, 10, 0, 0))] * 4


def table(scale, columns):
    return jnp.asarray((scale * MAIN[:, columns]).astype(np.float32), BF16)


def trace_call(sec, field, trow, tcol):
    comps = 10 + (sec == 0)
    return pl.pallas_call(
        partial(trace_kernel, sec),
        grid=(2,),
        in_specs=[field_spec(), whole((8, 256)), whole((256, 128)), whole((96, 192))],
        out_specs=[halo_spec(comps)] * 4,
        out_shape=[shape(2, comps, 16, 256)] * 4,
        compiler_params=params(16),
        cost_estimate=estimate(2),
        name="traces",
    )(far(field), trow, tcol, jnp.asarray(TRACE))


def first_section(field, req, resp, trow, tcol, halos):
    return pl.pallas_call(
        first_section_kernel,
        grid=(2,),
        in_specs=[field_spec(), whole((384, 128)), whole((128, 128)), whole((8, 256)), whole((256, 128))]
        + [whole((64, 256)), whole((96, 192))]
        + [halo_spec(10)] * 4
        + info_specs(),
        out_specs=[field_spec(), field_spec(), whole((128, 128))],
        out_shape=[pltpu.HBM(FIELD, F32), pltpu.HBM(FIELD, F32), shape(128, 128)],
        scratch_shapes=[
            vmem(10, 2, 64, 256),
            vmem(128, 128),
            vmem(640, 512, dtype=BF16),
            vmem(10, 2, 32, 256),
            vmem(10, 2, 32, 256),
            vmem(10, 2, 32, 256),
            vmem(4, 10, 16, 256),
            vmem(10, 3, 16, 256),
            vmem(10, 2, 32, 256, dtype=BF16),
            vmem(10, 2, 32, 256, dtype=BF16),
            vmem(10, 2, 192, 256, dtype=BF16),
            vmem(384, 128),
            vmem(640, 256),
        ],
        compiler_params=params(28),
        cost_estimate=estimate(10),
        name="first_section",
    )(far(field), req, resp, trow, tcol, table(-DT, slice(0, 256)), jnp.asarray(TRACE), *halos, *halos)


def inner(field, first, resp, trow, tcol):
    side_spec = pl.BlockSpec((1, 10, 2, 32, 256), lambda g: (g, 0, 0, 0, 0))
    return pl.pallas_call(
        inner_kernel,
        grid=(2,),
        in_specs=[field_spec(), field_spec(), whole((128, 128)), whole((8, 256)), whole((256, 128))]
        + [whole((64, 224)), whole((96, 192))],
        out_specs=[field_spec(), side_spec, side_spec],
        out_shape=[shape(*FIELD), shape(2, 10, 2, 32, 256), shape(2, 10, 2, 32, 256)],
        scratch_shapes=[
            vmem(10, 2, 64, 256),
            vmem(128, 128),
            vmem(640, 512, dtype=BF16),
            vmem(10, 2, 32, 256),
            vmem(10, 2, 32, 256, dtype=BF16),
            vmem(10, 2, 192, 256, dtype=BF16),
        ],
        compiler_params=params(24),
        cost_estimate=estimate(100),
        name="inner",
    )(far(field), far(first), resp, trow, tcol, table(-0.5 * DT, slice(0, 224)), jnp.asarray(TRACE))


def outer(part, xt, yt, resp, halos, infos):
    side_spec = pl.BlockSpec((1, 10, 2, 32, 256), lambda g: (g, 0, 0, 0, 0))
    return pl.pallas_call(
        outer_kernel,
        grid=(2,),
        in_specs=[field_spec(), side_spec, side_spec, whole((128, 128)), whole((64, 32))]
        + [halo_spec(10)] * 4
        + info_specs(),
        out_specs=field_spec(),
        out_shape=shape(*FIELD),
        scratch_shapes=[
            vmem(128, 128),
            vmem(4, 10, 16, 256),
            vmem(10, 3, 16, 256),
            vmem(10, 2, 32, 256, dtype=BF16),
        ],
        compiler_params=params(24),
        cost_estimate=estimate(10),
        name="outer",
    )(part, xt, yt, resp, table(-0.5 * DT, slice(224, 256)), *halos, *infos)


def on_device(field, owner, donor, target, weight):
    req, trow, tcol = pl.pallas_call(
        request_kernel,
        out_shape=[shape(384, 128), shape(8, 256), shape(256, 128)],
        compiler_params=pltpu.CompilerParams(vmem_limit_bytes=16 * 2**20),
        name="request",
    )(
        far(owner.reshape(2, DEV)),
        far(donor.reshape(2, DEV)),
        far(target.reshape(2, DEV)),
        far(jnp.swapaxes(weight[0, 0], 1, 2)),
    )
    req = exchange(req)
    infos = to_neighbours(trace_call(0, field, trow, tcol))
    resp = pl.pallas_call(
        interpolate_kernel,
        grid=(4,),
        in_specs=[
            pl.BlockSpec((2, 5, 1, 1, 64, 256), lambda i: (0, 0, i // 2, i % 2, 0, 0)),
            whole((384, 128)),
        ],
        out_specs=whole((128, 128)),
        out_shape=shape(128, 128),
        scratch_shapes=[vmem(384, 128), vmem(640, 256)],
        compiler_params=params(16),
        cost_estimate=estimate(100),
        name="interpolate",
    )(far(field), req)
    resp = exchange(resp)
    first, middle, resp = first_section(field, req, resp, trow, tcol, infos)
    resp = exchange(resp)
    halos = to_neighbours(trace_call(1, middle, trow, tcol))
    part, xt, yt = inner(middle, first, resp, trow, tcol)
    return outer(part, xt, yt, resp, halos, infos)


def solution(mesh):
    placed = (
        P(None, None, None, "rotor", None, "tower"),
        P("rotor", "tower", None, None, None),
        P("rotor", "tower", None, None),
        P("rotor", "tower", None, None),
        P("rotor", "tower", None, None, None),
    )
    return jax.shard_map(
        on_device,
        mesh=mesh,
        in_specs=placed,
        out_specs=P(None, None, None, "rotor", None, "tower"),
        check_vma=False,
    )
```

```python
from functools import partial

import jax
import jax.numpy as jnp
import numpy as np
from jax import lax
from jax.experimental import pallas as pl
from jax.experimental.pallas import tpu as pltpu
from jax.sharding import PartitionSpec as P

DT = 0.01
DEV = 128
AXES = ("rotor", "tower")
F32, BF16, I32 = jnp.float32, jnp.bfloat16, jnp.int32
HIGH = lax.Precision.HIGHEST


def lagrange_values(nodes, at):
    values = np.ones(4)
    for j in range(4):
        for m in range(4):
            if m != j:
                values[j] *= (at - nodes[m]) / (nodes[j] - nodes[m])
    return values


def lagrange_slopes(nodes, at):
    slopes = np.zeros(4)
    for j in range(4):
        for k in range(4):
            if k != j:
                factor = 1.0 / (nodes[j] - nodes[k])
                for m in range(4):
                    if m != j and m != k:
                        factor *= (at - nodes[m]) / (nodes[j] - nodes[m])
                slopes[j] += factor
    return slopes


def expand(block, axis):
    pieces = [np.eye(4)] * 3
    pieces[axis] = block
    return np.kron(np.kron(pieces[0], pieces[1]), pieces[2])


NODES = np.array([-0.8611363115940526, -0.3399810435848563, 0.3399810435848563, 0.8611363115940526])
QUAD = np.array([0.3478548451374538, 0.6521451548625461, 0.6521451548625461, 0.3478548451374538])
SLOPES = np.stack([lagrange_slopes(NODES, at) for at in NODES])
LOW, HIGHV = lagrange_values(NODES, -1.0), lagrange_values(NODES, 1.0)
LIFT_LO, LIFT_HI = LOW / QUAD, HIGHV / QUAD


def halves(table):
    hi = table.astype(np.float32).astype(jnp.bfloat16)
    lo = (table - hi.astype(np.float64)).astype(jnp.bfloat16)
    return hi, lo


def tables():
    e_lo = [expand(LOW[None, :], d) for d in range(3)]
    e_hi = [expand(HIGHV[None, :], d) for d in range(3)]
    l_lo = [expand(LIFT_LO[:, None], d) for d in range(3)]
    l_hi = [expand(LIFT_HI[:, None], d) for d in range(3)]
    weak = [expand(SLOPES, d) - l_hi[d] @ e_hi[d] + l_lo[d] @ e_lo[d] for d in range(3)]
    main = np.concatenate(weak + [-l_lo[2], l_hi[2], -l_lo[1], l_hi[1]], axis=1)
    trace = np.concatenate([t for d in range(3) for t in (e_lo[d], e_hi[d])], axis=0)
    t_hi, t_lo = halves(trace)
    return main, np.concatenate([t_hi, t_hi, t_lo], axis=1)


MAIN, TRACE = tables()


def iota(shape, dim):
    return lax.broadcasted_iota(I32, shape, dim)


def dot(a, b, precision=None):
    return lax.dot_general(a, b, (((1,), (0,)), ((), ())), precision=precision, preferred_element_type=F32)


def split(x):
    hi = x.astype(BF16)
    return hi, (x - hi.astype(F32)).astype(BF16)


def pick4(index, values):
    out = jnp.full(index.shape, float(values[3]), F32)
    for i in range(3):
        out = jnp.where(index == i, float(values[i]), out)
    return out


def primitive(u):
    rho, m1, m2, m3, en = u
    r = 1.0 / rho
    v = [m1 * r, m2 * r, m3 * r]
    vv = v[0] * v[0] + v[1] * v[1] + v[2] * v[2]
    p = 0.4 * (en - 0.5 * rho * vv)
    return r, v, vv, p


def tangent(du, r, v, vv):
    dv = [(du[1 + i] - v[i] * du[0]) * r for i in range(3)]
    dp = 0.4 * (du[4] - (v[0] * du[1] + v[1] * du[2] + v[2] * du[3]) + 0.5 * vv * du[0])
    return dv, dp


def flux(u, du, v, p, dv, dp, d):
    out = [u[1 + d]]
    dout = [du[1 + d]]
    for i in range(3):
        f = u[1 + i] * v[d]
        df = du[1 + i] * v[d] + u[1 + i] * dv[d]
        if i == d:
            f, df = f + (p - 1.0), df + dp
        out.append(f)
        dout.append(df)
    out.append((u[4] + p) * v[d])
    dout.append((du[4] + dp) * v[d] + (u[4] + p) * dv[d])
    return out, dout


def side(w, d):
    u, du = w[:5], w[5:]
    r, v, vv, p = primitive(u)
    dv, dp = tangent(du, r, v, vv)
    f, df = flux(u, du, v, p, dv, dp, d)
    c2 = 1.4 * p * r
    dc2 = 1.4 * r * dp - c2 * r * du[0]
    s2 = v[d] * v[d] + c2
    r1, r2 = lax.rsqrt(c2), lax.rsqrt(s2)
    s = c2 * r1 + s2 * r2
    ds = 0.5 * dc2 * r1 + (v[d] * dv[d] + 0.5 * dc2) * r2
    return f + df, s, ds


def common(left, right, d):
    fl, sl, dsl = side(left, d)
    fr, sr, dsr = side(right, d)
    s, ds = 0.25 * (sl + sr), 0.25 * (dsl + dsr)
    out = []
    for i in range(5):
        out.append(0.5 * (fl[i] + fr[i]) - s * (right[i] - left[i]))
    for i in range(5):
        out.append(
            0.5 * (fl[5 + i] + fr[5 + i]) - ds * (right[i] - left[i]) - s * (right[5 + i] - left[5 + i])
        )
    return out, fl, fr


def request_kernel(owner, donor, target, weight, req, trow, tcol):
    sub, lane = iota((DEV, DEV), 0), iota((DEV, DEV), 1)
    results = []
    tc = [jnp.zeros((DEV, DEV), F32) for _ in range(2)]
    for sec in range(2):
        orow = jnp.broadcast_to(owner[sec : sec + 1].astype(F32), (DEV, DEV))
        oc = orow.T
        same = (oc == orow) & (sub < lane)
        pos = jnp.sum(jnp.where(same, 1.0, 0.0), axis=0, keepdims=True)
        lists = [weight[sec], donor[sec : sec + 1].astype(F32), target[sec : sec + 1].astype(F32) + 1.0]
        rhs = jnp.concatenate(lists + [jnp.zeros((62, DEV), F32)], axis=0).T
        for s in range(2):
            chosen = (orow == sub.astype(F32)) & (pos == float(s))
            res = dot(jnp.where(chosen, 1.0, 0.0), rhs, HIGH)
            results.append(res)
            tc[s] = jnp.where(lane == sec, res[:, 65:66], tc[s])
    for sec in range(2):
        pair = jnp.where(lane < 64, results[2 * sec], pltpu.roll(results[2 * sec + 1], 64, 1))
        req[pl.ds(sec, DEV, stride=4), :] = pair
    ids = jnp.zeros((DEV, DEV), F32)
    for i in range(4):
        ids = jnp.where(lane == i, results[i][:, 64:65], ids)
    req[pl.ds(2, DEV, stride=4), :] = ids
    req[pl.ds(3, DEV, stride=4), :] = jnp.zeros((DEV, DEV), F32)
    for s in range(2):
        tcol[s * 128 : s * 128 + 128, :] = tc[s]
        trow[:, s * 128 : s * 128 + 128] = tc[s].T[0:8]


def block_in(field, buf, sem, i):
    return pltpu.make_async_copy(field.at[:, :, i // 2, i % 2], buf.at[i], sem.at[i])


def start_field(field, buf, sem):
    for i in range(4):
        block_in(field, buf, sem, i).start()


def point_row(trow, sec):
    return (trow[sec : sec + 1, :].astype(I32) - 1) >> 9


def element_col(tcol, sec, count):
    return jnp.broadcast_to((tcol[:, sec : sec + 1].astype(I32) - 1) & 511, (256, count))


def trace_kernel(sec, field, trow, tcol, xlo, xhi, ylo, yhi, buf, sem):
    start_field(field, buf, sem)
    upper = iota((8, 128), 0) < 4
    sides = [[jnp.where(upper, float(v[2 * k]), float(v[2 * k + 1])) for k in range(2)] for v in (LOW, HIGHV)]
    if sec == 0:
        info = jnp.concatenate([trow[0:2, :], jnp.ones((1, 256), F32), jnp.zeros((13, 256), F32)], axis=0)
        for out in (xlo, xhi, ylo, yhi):
            out[0, 10] = info
            out[1, 10] = jnp.zeros((16, 256), F32)
    for x in range(2):
        there = iota((256, 256), 1) + 256 * x == element_col(tcol, sec, 256)
        there = jnp.where(there, 1.0, 0.0).astype(BF16)
        for g in range(2):
            at = jnp.where(iota((64, 256), 0) + 64 * g == point_row(trow, sec), 1.0, 0.0).astype(BF16)
            keep = dot(at, there) < 0.5
            i = 2 * g + x
            block_in(field, buf, sem, i).wait()
            along, xout = ((LOW, xlo), (HIGHV, xhi))[x]
            lanes = slice(128 * x, 128 * x + 128)
            for c in range(10):
                w = jnp.where(keep, buf[i, c // 5, c % 5], 0.0)
                xout[g, c] = sum(float(along[a]) * w[16 * a : 16 * a + 16] for a in range(4))
                for y, out in ((0, ylo), (1, yhi)):
                    half = w[:, 128 * y : 128 * y + 128]
                    rows = []
                    for a in range(4):
                        t = sides[y][0] * half[16 * a : 16 * a + 8] + sides[y][1] * half[16 * a + 8 : 16 * a + 16]
                        rows.append(t + pltpu.roll(t, 4, 0))
                    for k in range(2):
                        out[g, c, 8 * k : 8 * k + 8, lanes] = jnp.where(upper, rows[2 * k], rows[2 * k + 1])


def load_asked(req, asked):
    for i in range(3):
        asked[i * 128 : i * 128 + 128, :] = req[pl.ds(i, DEV, stride=4), :].T


def pick(asked, sec, donors):
    ids = asked[256 + 2 * sec : 256 + 2 * sec + 2, :]
    row = jnp.concatenate([ids[0:1], ids[1:2]], axis=1).astype(I32)
    return dot(donors[...], jnp.where(iota((1024, 256), 0) == row, 1.0, 0.0).astype(BF16))


def answer(asked, sec, picks):
    w = jnp.concatenate([asked[sec * 128 : sec * 128 + 64], asked[sec * 128 + 64 : sec * 128 + 128]], axis=1)
    rows = [jnp.sum(picks[64 * c : 64 * c + 64, :] * w, axis=0, keepdims=True) for c in range(10)]
    value = jnp.concatenate(
        [r[:, 0:128] for r in rows]
        + [jnp.zeros((2, 128), F32)]
        + [r[:, 128:256] for r in rows]
        + [jnp.zeros((2, 128), F32)],
        axis=0,
    )
    groups = [value] + [pltpu.roll(value, by, 1) for by in (16, 112, 1, 127)] + [jnp.zeros((8, 128), F32)]
    return jnp.concatenate(groups, axis=0).T


def interpolate_kernel(field, req, resp, asked, picks, donors, buf, sem):
    start_field(field, buf, sem)
    load_asked(req, asked)
    for i in range(4):
        block_in(field, buf, sem, i).wait()
        for c in range(10):
            donors[64 * c : 64 * c + 64, 256 * i : 256 * i + 256] = buf[i, c // 5, c % 5].astype(BF16)
    picks[...] = pick(asked, 0, donors)
    resp[...] = answer(asked, 0, picks)


def values(got, j):
    both = got[24 * j : 24 * j + 24, :]
    return jnp.concatenate([both[0:10], both[12:22]], axis=1)


def set_fringe(field, buf, sem, got, trow, tcol, sec, g, lhs, now):
    val = values(got, 0)
    at = iota((64, 256), 0) + 64 * g == point_row(trow, sec)
    for c in range(10):
        hi, lo = split(jnp.where(at, val[c : c + 1], 0.0))
        lhs[64 * c : 64 * c + 64, 0:256] = hi
        lhs[64 * c : 64 * c + 64, 256:512] = lo
    where = jnp.where(iota((256, 512), 1) == element_col(tcol, sec, 512), 1.0, 0.0).astype(BF16)
    mask = dot(jnp.where(at, 1.0, 0.0).astype(BF16), where)
    for x in range(2):
        wx = where[:, x * 256 : x * 256 + 256]
        scat = dot(lhs[...], jnp.concatenate([wx, wx], axis=0))
        block_in(field, buf, sem, 2 * g + x).wait()
        hit = mask[:, x * 256 : x * 256 + 256] > 0.5
        for c in range(10):
            now[c, x] = jnp.where(hit, scat[64 * c : 64 * c + 64], buf[2 * g + x, c // 5, c % 5])


def all_traces(now, table, xt, yt, zt):
    for c in range(10):
        for x in range(2):
            hi, lo = split(now[c, x])
            res = dot(table[...], jnp.concatenate([hi, lo, hi], axis=0))
            xt[c, x] = res[0:32]
            yt[c, x] = res[32:64]
            zt[c, x] = res[64:96]


def mend_halos(halo, info, got, sec, g, xt, yt, hal):
    for j in range(4):
        k = (j + 2) % 4
        row2 = info[k][0, 10, sec : sec + 1, :]
        present = info[k][0, 10, 2:3, 0:128] > 0.5
        pt = (row2.astype(I32) - 1) >> 9
        q = pt & 63
        elem = (row2.astype(I32) - 1) & 511
        weights = HIGHV if j % 2 == 0 else LOW
        if j < 2:
            fp, coef = q & 15, pick4(q >> 4, weights)
            want = 1 if j == 0 else 0
            place = jnp.where((elem >> 8) == want, elem & 255, -1)
        else:
            fp, coef = ((q >> 4) << 2) | (q & 3), pick4((q >> 2) & 3, weights)
            want = 1 if j == 2 else 0
            place = jnp.where(((elem >> 7) & 1) == want, ((elem >> 8) << 7) | (elem & 127), -1)
        coef = jnp.where((pt >> 6) == g, coef, 0.0)
        nval = values(got, 1 + j) * coef
        hit = iota((16, 256), 0) == fp
        his, los = [], []
        for c in range(10):
            hi, lo = split(jnp.where(hit, nval[c : c + 1], 0.0))
            his.append(hi)
            los.append(lo)
        left = jnp.concatenate([jnp.concatenate(his, axis=0), jnp.concatenate(los, axis=0)], axis=1)
        pcol = jnp.broadcast_to(place.astype(F32), (128, 256)).T
        pcol = jnp.concatenate([pcol, pcol], axis=1)
        there = jnp.where(iota((256, 256), 1).astype(F32) == pcol, 1.0, 0.0).astype(BF16)
        fix = dot(left, jnp.concatenate([there, there], axis=0))
        own = slice(0, 16) if j % 2 == 0 else slice(16, 32)
        for c in range(10):
            for t in range(2):
                lanes = slice(128 * t, 128 * t + 128)
                theirs = halo[k][g, c, :, lanes] + fix[16 * c : 16 * c + 16, lanes]
                if j < 2:
                    mine = xt[c, j, own, lanes]
                else:
                    y = j - 2
                    mine = yt[c, t, own, 128 * y : 128 * y + 128]
                hal[j, c, :, lanes] = jnp.where(present, theirs, mine)


def faces_xy(xt, yt, hal, hx, hy):
    for face in range(3):
        for t in range(2):
            lanes = slice(128 * t, 128 * t + 128)
            left = [hal[0, c, :, lanes] if face == 0 else xt[c, face - 1, 16:32, lanes] for c in range(10)]
            right = [hal[1, c, :, lanes] if face == 2 else xt[c, face, 0:16, lanes] for c in range(10)]
            out, _, _ = common(left, right, 0)
            for c in range(10):
                hx[c, face, :, lanes] = out[c]
    for face in range(3):
        for x in range(2):
            mine = slice(128 * x, 128 * x + 128)
            before = slice(128 * face - 128, 128 * face)
            after = slice(128 * face, 128 * face + 128)
            left = [hal[2, c, :, mine] if face == 0 else yt[c, x, 16:32, before] for c in range(10)]
            right = [hal[3, c, :, mine] if face == 2 else yt[c, x, 0:16, after] for c in range(10)]
            out, _, _ = common(left, right, 1)
            for c in range(10):
                h = out[c].astype(BF16)
                if face < 2:
                    hy[c, x, 0:16, after] = h
                if face > 0:
                    hy[c, x, 16:32, before] = h


def faces_z(zt, hz):
    edge = iota((16, 128), 1) == 0
    for t in range(2):
        lanes = slice(128 * t, 128 * t + 128)
        for x in range(2):
            left = [pltpu.roll(zt[c, x, 16:32, lanes], 1, 1) for c in range(10)]
            right = [zt[c, x, 0:16, lanes] for c in range(10)]
            out, fl, fr = common(left, right, 2)
            for c in range(10):
                hz[c, x, 0:16, lanes] = jnp.where(edge, fr[c], out[c]).astype(BF16)
                hz[c, x, 16:32, lanes] = pltpu.roll(jnp.where(edge, fl[c], out[c]), 127, 1).astype(BF16)


def point_fluxes(now, vol):
    @pl.loop(0, 8, unroll=2)
    def _(i):
        x, q = i // 4, pl.multiple_of((i % 4) * 16, 16)
        for t in range(2):
            lanes = slice(128 * t, 128 * t + 128)
            w = [now[c, x, pl.ds(q, 16), lanes] for c in range(10)]
            u, du = w[:5], w[5:]
            r, v, vv, p = primitive(u)
            dv, dp = tangent(du, r, v, vv)
            for d in range(3):
                f, df = flux(u, du, v, p, dv, dp, d)
                for c in range(10):
                    vol[c, x, pl.ds(64 * d + q, 16), lanes] = (f + df)[c].astype(BF16)


def lift_x(hx, c, x, a, scale):
    return float(-scale * LIFT_HI[a]) * hx[c, x + 1] + float(scale * LIFT_LO[a]) * hx[c, x]


def blocks_out(src, dst, sem, g, x):
    return [
        pltpu.make_async_copy(src.at[g, pl.ds(5 * f, 5), x], dst.at[f, :, g, x], sem.at[g, x, f]) for f in range(2)
    ]


def first_section_kernel(field, req, resp, trow, tcol, main_t, trace_t, *refs):
    halo, info, (now_out, mid_out, resp_out), scratch = refs[0:4], refs[4:8], refs[8:11], refs[11:]
    nows, mids, got, lhs, xt, yt, zt, hal, hx, hy, hz, vol, asked, picks, donors, buf, sem, nsem, msem = scratch
    g = pl.program_id(0)
    now, mid = nows.at[g], mids.at[g]

    @pl.when(g == 0)
    def _():
        start_field(field, buf, sem)
        got[...] = resp[...].T
        load_asked(req, asked)

    set_fringe(field, buf, sem, got, trow, tcol, 0, g, lhs, now)
    for x in range(2):
        for copy in blocks_out(nows, now_out, nsem, g, x):
            copy.start()
    all_traces(now, trace_t, xt, yt, zt)
    mend_halos(halo, info, got, 0, g, xt, yt, hal)
    faces_xy(xt, yt, hal, hx, hy)
    faces_z(zt, hz)
    point_fluxes(now, vol)
    for x in range(2):
        columns = pl.ds(pl.multiple_of(512 * g + 256 * x, 256), 256)
        for c in range(10):
            res = dot(main_t[...], jnp.concatenate([vol[c, x], hz[c, x], hy[c, x]], axis=0))
            for a in range(4):
                rows = slice(16 * a, 16 * a + 16)
                new = now[c, x, rows] + (res[rows] + lift_x(hx, c, x, a, DT))
                mid[c, x, rows] = new
                donors[64 * c + 16 * a : 64 * c + 16 * a + 16, columns] = new.astype(BF16)
        for copy in blocks_out(mids, mid_out, msem, g, x):
            copy.start()

    @pl.when(g == 1)
    def _():
        picks[...] = pick(asked, 1, donors)
        resp_out[...] = answer(asked, 1, picks)
        for h in range(2):
            for x in range(2):
                for copy in blocks_out(nows, now_out, nsem, h, x) + blocks_out(mids, mid_out, msem, h, x):
                    copy.wait()


def inner_kernel(field, resp, trow, tcol, main_t, trace_t, partial_out, xt_out, yt_out, *scratch):
    now, got, lhs, zt, hz, vol, buf, sem = scratch
    g = pl.program_id(0)

    @pl.when(g == 0)
    def _():
        start_field(field, buf, sem)
        got[...] = resp[...].T

    set_fringe(field, buf, sem, got, trow, tcol, 1, g, lhs, now)
    all_traces(now, trace_t, xt_out.at[g], yt_out.at[g], zt)
    faces_z(zt, hz)
    point_fluxes(now, vol)
    for x in range(2):
        for c in range(10):
            res = dot(main_t[...], jnp.concatenate([vol[c, x], hz[c, x]], axis=0))
            partial_out[c // 5, c % 5, g, x] = 0.5 * now[c, x] + res


def outer_kernel(part, first, xt, yt, resp, lift_y, *refs):
    halo, info, result, (got, hal, hx, hy) = refs[0:4], refs[4:8], refs[8], refs[9:]
    g = pl.program_id(0)

    @pl.when(g == 0)
    def _():
        got[...] = resp[...].T

    mend_halos(halo, info, got, 1, g, xt.at[g], yt.at[g], hal)
    faces_xy(xt.at[g], yt.at[g], hal, hx, hy)
    for x in range(2):
        for c in range(10):
            res = dot(lift_y[...], hy[c, x])
            for a in range(4):
                rows = slice(16 * a, 16 * a + 16)
                add = res[rows] + lift_x(hx, c, x, a, 0.5 * DT)
                base = part[c // 5, c % 5, g, x, rows] + 0.5 * first[c // 5, c % 5, g, x, rows]
                result[c // 5, c % 5, 0, x, rows] = base + add


FIELD = (2, 5, 2, 2, 64, 256)


def field_spec():
    return pl.BlockSpec((2, 5, 1, 2, 64, 256), lambda g: (0, 0, g, 0, 0, 0))


HERE = pl.BlockSpec(memory_space=pltpu.VMEM)
AWAY = pl.BlockSpec(memory_space=pl.ANY)


def blocks():
    return [pltpu.VMEM((4, 2, 5, 64, 256), F32), pltpu.SemaphoreType.DMA((4,))]


def shape(*dims):
    return jax.ShapeDtypeStruct(dims, F32)


def params(mb):
    return pltpu.CompilerParams(dimension_semantics=("arbitrary",), vmem_limit_bytes=mb * 2**20)


def shift(x, axis, up):
    n = lax.axis_size(axis)
    pairs = [(i, i + 1) if up else (i + 1, i) for i in range(n - 1)]
    return lax.ppermute(x, axis, pairs)


def to_neighbours(traces):
    xlo, xhi, ylo, yhi = traces
    y = [shift(yhi, "tower", True), shift(ylo, "tower", False)]
    return y + [shift(xhi, "rotor", True), shift(xlo, "rotor", False)]


def exchange(x):
    return lax.all_to_all(x, AXES, split_axis=0, concat_axis=0, tiled=True)


def estimate(us):
    return pl.CostEstimate(flops=int(us * 10**9), bytes_accessed=10**5, transcendentals=0)


def vmem(*dims, dtype=F32):
    return pltpu.VMEM(dims, dtype)


def far(x):
    return pltpu.with_memory_space_constraint(x, pltpu.HBM)


def table(scale, columns):
    return jnp.asarray((scale * MAIN[:, columns]).astype(np.float32), BF16)


def trace_call(sec, field, trow, tcol):
    comps = 10 + (sec == 0)
    return pl.pallas_call(
        partial(trace_kernel, sec),
        in_specs=[AWAY, HERE, HERE],
        out_specs=[HERE] * 4,
        out_shape=[shape(2, comps, 16, 256)] * 4,
        scratch_shapes=blocks(),
        compiler_params=pltpu.CompilerParams(vmem_limit_bytes=16 * 2**20),
        cost_estimate=estimate(2),
        name="traces",
    )(far(field), trow, tcol)


def first_section(field, req, resp, trow, tcol, halos):
    return pl.pallas_call(
        first_section_kernel,
        grid=(2,),
        in_specs=[AWAY] + [HERE] * 14,
        out_specs=[AWAY, AWAY, HERE],
        out_shape=[pltpu.HBM(FIELD, F32), pltpu.HBM(FIELD, F32), shape(128, 128)],
        scratch_shapes=[
            vmem(2, 10, 2, 64, 256),
            vmem(2, 10, 2, 64, 256),
            vmem(128, 128),
            vmem(640, 512, dtype=BF16),
            vmem(10, 2, 32, 256),
            vmem(10, 2, 32, 256),
            vmem(10, 2, 32, 256),
            vmem(4, 10, 16, 256),
            vmem(10, 3, 16, 256),
            vmem(10, 2, 32, 256, dtype=BF16),
            vmem(10, 2, 32, 256, dtype=BF16),
            vmem(10, 2, 192, 256, dtype=BF16),
            vmem(384, 128),
            vmem(640, 256),
            vmem(640, 1024, dtype=BF16),
            *blocks(),
            pltpu.SemaphoreType.DMA((2, 2, 2)),
            pltpu.SemaphoreType.DMA((2, 2, 2)),
        ],
        compiler_params=params(28),
        cost_estimate=estimate(10),
        name="first_section",
    )(far(field), req, resp, trow, tcol, table(-DT, slice(0, 256)), jnp.asarray(TRACE), *halos, *halos)


def inner(field, resp, trow, tcol):
    return pl.pallas_call(
        inner_kernel,
        grid=(2,),
        in_specs=[AWAY] + [HERE] * 5,
        out_specs=[HERE] * 3,
        out_shape=[shape(*FIELD), shape(2, 10, 2, 32, 256), shape(2, 10, 2, 32, 256)],
        scratch_shapes=[
            vmem(10, 2, 64, 256),
            vmem(128, 128),
            vmem(640, 512, dtype=BF16),
            vmem(10, 2, 32, 256),
            vmem(10, 2, 32, 256, dtype=BF16),
            vmem(10, 2, 192, 256, dtype=BF16),
            *blocks(),
        ],
        compiler_params=params(24),
        cost_estimate=estimate(100),
        name="inner",
    )(far(field), resp, trow, tcol, table(-0.5 * DT, slice(0, 224)), jnp.asarray(TRACE))


def outer(part, first, xt, yt, resp, halos, infos):
    return pl.pallas_call(
        outer_kernel,
        grid=(2,),
        in_specs=[HERE] * 14,
        out_specs=field_spec(),
        out_shape=shape(*FIELD),
        scratch_shapes=[
            vmem(128, 128),
            vmem(4, 10, 16, 256),
            vmem(10, 3, 16, 256),
            vmem(10, 2, 32, 256, dtype=BF16),
        ],
        compiler_params=params(24),
        cost_estimate=estimate(10),
        name="outer",
    )(part, first, xt, yt, resp, table(-0.5 * DT, slice(224, 256)), *halos, *infos)


def on_device(field, owner, donor, target, weight):
    req, trow, tcol = pl.pallas_call(
        request_kernel,
        out_shape=[shape(512, 128), shape(8, 256), shape(256, 128)],
        compiler_params=pltpu.CompilerParams(vmem_limit_bytes=16 * 2**20),
        name="request",
    )(
        far(owner.reshape(2, DEV)),
        far(donor.reshape(2, DEV)),
        far(target.reshape(2, DEV)),
        far(jnp.swapaxes(weight[0, 0], 1, 2)),
    )
    req = exchange(req)
    infos = to_neighbours(trace_call(0, field, trow, tcol))
    resp = pl.pallas_call(
        interpolate_kernel,
        in_specs=[AWAY, HERE],
        out_specs=HERE,
        out_shape=shape(128, 128),
        scratch_shapes=[vmem(384, 128), vmem(640, 256), vmem(640, 1024, dtype=BF16)] + blocks(),
        compiler_params=pltpu.CompilerParams(vmem_limit_bytes=16 * 2**20),
        cost_estimate=estimate(100),
        name="interpolate",
    )(far(field), req)
    resp = exchange(resp)
    first, middle, resp = first_section(field, req, resp, trow, tcol, infos)
    resp = exchange(resp)
    halos = to_neighbours(trace_call(1, middle, trow, tcol))
    part, xt, yt = inner(middle, resp, trow, tcol)
    return outer(part, first, xt, yt, resp, halos, infos)


def solution(mesh):
    placed = (
        P(None, None, None, "rotor", None, "tower"),
        P("rotor", "tower", None, None, None),
        P("rotor", "tower", None, None),
        P("rotor", "tower", None, None),
        P("rotor", "tower", None, None, None),
    )
    return jax.shard_map(
        on_device,
        mesh=mesh,
        in_specs=placed,
        out_specs=P(None, None, None, "rotor", None, "tower"),
        check_vma=False,
    )
```

```python
from functools import partial

import jax
import jax.numpy as jnp
import numpy as np
from jax import lax
from jax.experimental import pallas as pl
from jax.experimental.pallas import tpu as pltpu
from jax.sharding import PartitionSpec as P

DT = 0.01
DEV = 128
AXES = ("rotor", "tower")
F32, BF16, I32 = jnp.float32, jnp.bfloat16, jnp.int32
HIGH = lax.Precision.HIGHEST


def lagrange_values(nodes, at):
    values = np.ones(4)
    for j in range(4):
        for m in range(4):
            if m != j:
                values[j] *= (at - nodes[m]) / (nodes[j] - nodes[m])
    return values


def lagrange_slopes(nodes, at):
    slopes = np.zeros(4)
    for j in range(4):
        for k in range(4):
            if k != j:
                factor = 1.0 / (nodes[j] - nodes[k])
                for m in range(4):
                    if m != j and m != k:
                        factor *= (at - nodes[m]) / (nodes[j] - nodes[m])
                slopes[j] += factor
    return slopes


def expand(block, axis):
    pieces = [np.eye(4)] * 3
    pieces[axis] = block
    return np.kron(np.kron(pieces[0], pieces[1]), pieces[2])


NODES = np.array([-0.8611363115940526, -0.3399810435848563, 0.3399810435848563, 0.8611363115940526])
QUAD = np.array([0.3478548451374538, 0.6521451548625461, 0.6521451548625461, 0.3478548451374538])
SLOPES = np.stack([lagrange_slopes(NODES, at) for at in NODES])
LOW, HIGHV = lagrange_values(NODES, -1.0), lagrange_values(NODES, 1.0)
LIFT_LO, LIFT_HI = LOW / QUAD, HIGHV / QUAD


def halves(table):
    hi = table.astype(np.float32).astype(jnp.bfloat16)
    lo = (table - hi.astype(np.float64)).astype(jnp.bfloat16)
    return hi, lo


def tables():
    e_lo = [expand(LOW[None, :], d) for d in range(3)]
    e_hi = [expand(HIGHV[None, :], d) for d in range(3)]
    l_lo = [expand(LIFT_LO[:, None], d) for d in range(3)]
    l_hi = [expand(LIFT_HI[:, None], d) for d in range(3)]
    weak = [expand(SLOPES, d) - l_hi[d] @ e_hi[d] + l_lo[d] @ e_lo[d] for d in range(3)]
    main = np.concatenate(weak + [-l_lo[2], l_hi[2], -l_lo[1], l_hi[1]], axis=1)
    trace = np.concatenate([t for d in range(3) for t in (e_lo[d], e_hi[d])], axis=0)
    t_hi, t_lo = halves(trace)
    return main, np.concatenate([t_hi, t_hi, t_lo], axis=1)


MAIN, TRACE = tables()


def iota(shape, dim):
    return lax.broadcasted_iota(I32, shape, dim)


def dot(a, b, precision=None):
    return lax.dot_general(a, b, (((1,), (0,)), ((), ())), precision=precision, preferred_element_type=F32)


def split(x):
    hi = x.astype(BF16)
    return hi, (x - hi.astype(F32)).astype(BF16)


def pick4(index, values):
    out = jnp.full(index.shape, float(values[3]), F32)
    for i in range(3):
        out = jnp.where(index == i, float(values[i]), out)
    return out


def primitive(u):
    rho, m1, m2, m3, en = u
    r = 1.0 / rho
    v = [m1 * r, m2 * r, m3 * r]
    vv = v[0] * v[0] + v[1] * v[1] + v[2] * v[2]
    p = 0.4 * (en - 0.5 * rho * vv)
    return r, v, vv, p


def tangent(du, r, v, vv):
    dv = [(du[1 + i] - v[i] * du[0]) * r for i in range(3)]
    dp = 0.4 * (du[4] - (v[0] * du[1] + v[1] * du[2] + v[2] * du[3]) + 0.5 * vv * du[0])
    return dv, dp


def flux(u, du, v, p, dv, dp, d):
    out = [u[1 + d]]
    dout = [du[1 + d]]
    for i in range(3):
        f = u[1 + i] * v[d]
        df = du[1 + i] * v[d] + u[1 + i] * dv[d]
        if i == d:
            f, df = f + (p - 1.0), df + dp
        out.append(f)
        dout.append(df)
    out.append((u[4] + p) * v[d])
    dout.append((du[4] + dp) * v[d] + (u[4] + p) * dv[d])
    return out, dout


def side(w, d):
    u, du = w[:5], w[5:]
    r, v, vv, p = primitive(u)
    dv, dp = tangent(du, r, v, vv)
    f, df = flux(u, du, v, p, dv, dp, d)
    c2 = 1.4 * p * r
    dc2 = 1.4 * r * dp - c2 * r * du[0]
    s2 = v[d] * v[d] + c2
    r1, r2 = lax.rsqrt(c2), lax.rsqrt(s2)
    s = c2 * r1 + s2 * r2
    ds = 0.5 * dc2 * r1 + (v[d] * dv[d] + 0.5 * dc2) * r2
    return f + df, s, ds


def common(left, right, d):
    fl, sl, dsl = side(left, d)
    fr, sr, dsr = side(right, d)
    s, ds = 0.25 * (sl + sr), 0.25 * (dsl + dsr)
    out = []
    for i in range(5):
        out.append(0.5 * (fl[i] + fr[i]) - s * (right[i] - left[i]))
    for i in range(5):
        out.append(
            0.5 * (fl[5 + i] + fr[5 + i]) - ds * (right[i] - left[i]) - s * (right[5 + i] - left[5 + i])
        )
    return out, fl, fr


def request_kernel(owner, donor, target, weight, req, trow, tcol):
    sub, lane = iota((DEV, DEV), 0), iota((DEV, DEV), 1)
    results = []
    tc = [jnp.zeros((DEV, DEV), F32) for _ in range(2)]
    for sec in range(2):
        orow = jnp.broadcast_to(owner[sec : sec + 1].astype(F32), (DEV, DEV))
        oc = orow.T
        same = (oc == orow) & (sub < lane)
        pos = jnp.sum(jnp.where(same, 1.0, 0.0), axis=0, keepdims=True)
        lists = [weight[sec], donor[sec : sec + 1].astype(F32), target[sec : sec + 1].astype(F32) + 1.0]
        rhs = jnp.concatenate(lists + [jnp.zeros((62, DEV), F32)], axis=0).T
        for s in range(2):
            chosen = (orow == sub.astype(F32)) & (pos == float(s))
            res = dot(jnp.where(chosen, 1.0, 0.0), rhs, HIGH)
            results.append(res)
            tc[s] = jnp.where(lane == sec, res[:, 65:66], tc[s])
    for sec in range(2):
        pair = jnp.where(lane < 64, results[2 * sec], pltpu.roll(results[2 * sec + 1], 64, 1))
        req[pl.ds(sec, DEV, stride=4), :] = pair
    ids = jnp.zeros((DEV, DEV), F32)
    for i in range(4):
        ids = jnp.where(lane == i, results[i][:, 64:65], ids)
    req[pl.ds(2, DEV, stride=4), :] = ids
    req[pl.ds(3, DEV, stride=4), :] = jnp.zeros((DEV, DEV), F32)
    for s in range(2):
        tcol[s * 128 : s * 128 + 128, :] = tc[s]
        trow[:, s * 128 : s * 128 + 128] = tc[s].T[0:8]


def block_in(field, buf, sem, i):
    return pltpu.make_async_copy(field.at[:, :, i // 2, i % 2], buf.at[i], sem.at[i])


def start_field(field, buf, sem):
    for i in range(4):
        block_in(field, buf, sem, i).start()


def point_row(trow, sec):
    return (trow[sec : sec + 1, :].astype(I32) - 1) >> 9


def element_col(tcol, sec, count):
    return jnp.broadcast_to((tcol[:, sec : sec + 1].astype(I32) - 1) & 511, (256, count))


def trace_kernel(sec, field, trow, tcol, xlo, xhi, ylo, yhi, buf, sem):
    start_field(field, buf, sem)
    upper = iota((8, 128), 0) < 4
    sides = [[jnp.where(upper, float(v[2 * k]), float(v[2 * k + 1])) for k in range(2)] for v in (LOW, HIGHV)]
    if sec == 0:
        info = jnp.concatenate([trow[0:2, :], jnp.ones((1, 256), F32), jnp.zeros((13, 256), F32)], axis=0)
        for out in (xlo, xhi, ylo, yhi):
            out[0, 10] = info
            out[1, 10] = jnp.zeros((16, 256), F32)
    for x in range(2):
        there = iota((256, 256), 1) + 256 * x == element_col(tcol, sec, 256)
        there = jnp.where(there, 1.0, 0.0).astype(BF16)
        for g in range(2):
            at = jnp.where(iota((64, 256), 0) + 64 * g == point_row(trow, sec), 1.0, 0.0).astype(BF16)
            keep = dot(at, there) < 0.5
            i = 2 * g + x
            block_in(field, buf, sem, i).wait()
            along, xout = ((LOW, xlo), (HIGHV, xhi))[x]
            lanes = slice(128 * x, 128 * x + 128)
            for c in range(10):
                w = jnp.where(keep, buf[i, c // 5, c % 5], 0.0)
                xout[g, c] = sum(float(along[a]) * w[16 * a : 16 * a + 16] for a in range(4))
                for y, out in ((0, ylo), (1, yhi)):
                    half = w[:, 128 * y : 128 * y + 128]
                    rows = []
                    for a in range(4):
                        t = sides[y][0] * half[16 * a : 16 * a + 8] + sides[y][1] * half[16 * a + 8 : 16 * a + 16]
                        rows.append(t + pltpu.roll(t, 4, 0))
                    for k in range(2):
                        out[g, c, 8 * k : 8 * k + 8, lanes] = jnp.where(upper, rows[2 * k], rows[2 * k + 1])


def load_asked(req, asked):
    for i in range(3):
        asked[i * 128 : i * 128 + 128, :] = req[pl.ds(i, DEV, stride=4), :].T


def pick(asked, sec, donors):
    ids = asked[256 + 2 * sec : 256 + 2 * sec + 2, :]
    row = jnp.concatenate([ids[0:1], ids[1:2]], axis=1).astype(I32)
    return dot(donors[...], jnp.where(iota((1024, 256), 0) == row, 1.0, 0.0).astype(BF16))


def answer(asked, sec, picks):
    w = jnp.concatenate([asked[sec * 128 : sec * 128 + 64], asked[sec * 128 + 64 : sec * 128 + 128]], axis=1)
    rows = [jnp.sum(picks[64 * c : 64 * c + 64, :] * w, axis=0, keepdims=True) for c in range(10)]
    value = jnp.concatenate(
        [r[:, 0:128] for r in rows]
        + [jnp.zeros((2, 128), F32)]
        + [r[:, 128:256] for r in rows]
        + [jnp.zeros((2, 128), F32)],
        axis=0,
    )
    groups = [value] + [pltpu.roll(value, by, 1) for by in (16, 112, 1, 127)] + [jnp.zeros((8, 128), F32)]
    return jnp.concatenate(groups, axis=0).T


def interpolate_kernel(field, req, resp, asked, picks, donors, buf, sem):
    start_field(field, buf, sem)
    load_asked(req, asked)
    for i in range(4):
        block_in(field, buf, sem, i).wait()
        for c in range(10):
            donors[64 * c : 64 * c + 64, 256 * i : 256 * i + 256] = buf[i, c // 5, c % 5].astype(BF16)
    picks[...] = pick(asked, 0, donors)
    resp[...] = answer(asked, 0, picks)


def values(got, j):
    both = got[24 * j : 24 * j + 24, :]
    return jnp.concatenate([both[0:10], both[12:22]], axis=1)


def set_fringe(field, buf, sem, got, trow, tcol, sec, g, lhs, now):
    val = values(got, 0)
    at = iota((64, 256), 0) + 64 * g == point_row(trow, sec)
    for c in range(10):
        lhs[64 * c : 64 * c + 64, :] = jnp.where(at, val[c : c + 1], 0.0).astype(BF16)
    where = jnp.where(iota((256, 512), 1) == element_col(tcol, sec, 512), 1.0, 0.0).astype(BF16)
    mask = dot(jnp.where(at, 1.0, 0.0).astype(BF16), where)
    for x in range(2):
        wx = where[:, x * 256 : x * 256 + 256]
        scat = dot(lhs[...], wx)
        block_in(field, buf, sem, 2 * g + x).wait()
        hit = mask[:, x * 256 : x * 256 + 256] > 0.5
        for c in range(10):
            now[c, x] = jnp.where(hit, scat[64 * c : 64 * c + 64], buf[2 * g + x, c // 5, c % 5])


def all_traces(now, table, xt, yt, zt):
    for c in range(10):
        for x in range(2):
            hi, lo = split(now[c, x])
            res = dot(table[...], jnp.concatenate([hi, lo, hi], axis=0))
            xt[c, x] = res[0:32]
            yt[c, x] = res[32:64]
            zt[c, x] = res[64:96]


def mend_halos(halo, info, got, sec, g, xt, yt, hal):
    for j in range(4):
        k = (j + 2) % 4
        row2 = info[k][0, 10, sec : sec + 1, :]
        present = info[k][0, 10, 2:3, 0:128] > 0.5
        pt = (row2.astype(I32) - 1) >> 9
        q = pt & 63
        elem = (row2.astype(I32) - 1) & 511
        weights = HIGHV if j % 2 == 0 else LOW
        if j < 2:
            fp, coef = q & 15, pick4(q >> 4, weights)
            want = 1 if j == 0 else 0
            place = jnp.where((elem >> 8) == want, elem & 255, -1)
        else:
            fp, coef = ((q >> 4) << 2) | (q & 3), pick4((q >> 2) & 3, weights)
            want = 1 if j == 2 else 0
            place = jnp.where(((elem >> 7) & 1) == want, ((elem >> 8) << 7) | (elem & 127), -1)
        coef = jnp.where((pt >> 6) == g, coef, 0.0)
        nval = values(got, 1 + j) * coef
        hit = iota((16, 256), 0) == fp
        his, los = [], []
        for c in range(10):
            hi, lo = split(jnp.where(hit, nval[c : c + 1], 0.0))
            his.append(hi)
            los.append(lo)
        left = jnp.concatenate([jnp.concatenate(his, axis=0), jnp.concatenate(los, axis=0)], axis=1)
        pcol = jnp.broadcast_to(place.astype(F32), (128, 256)).T
        pcol = jnp.concatenate([pcol, pcol], axis=1)
        there = jnp.where(iota((256, 256), 1).astype(F32) == pcol, 1.0, 0.0).astype(BF16)
        fix = dot(left, jnp.concatenate([there, there], axis=0))
        own = slice(0, 16) if j % 2 == 0 else slice(16, 32)
        for c in range(10):
            for t in range(2):
                lanes = slice(128 * t, 128 * t + 128)
                theirs = halo[k][g, c, :, lanes] + fix[16 * c : 16 * c + 16, lanes]
                if j < 2:
                    mine = xt[c, j, own, lanes]
                else:
                    y = j - 2
                    mine = yt[c, t, own, 128 * y : 128 * y + 128]
                hal[j, c, :, lanes] = jnp.where(present, theirs, mine)


def faces_xy(xt, yt, hal, hx, hy):
    for face in range(3):
        for t in range(2):
            lanes = slice(128 * t, 128 * t + 128)
            left = [hal[0, c, :, lanes] if face == 0 else xt[c, face - 1, 16:32, lanes] for c in range(10)]
            right = [hal[1, c, :, lanes] if face == 2 else xt[c, face, 0:16, lanes] for c in range(10)]
            out, _, _ = common(left, right, 0)
            for c in range(10):
                hx[c, face, :, lanes] = out[c]
    for face in range(3):
        for x in range(2):
            mine = slice(128 * x, 128 * x + 128)
            before = slice(128 * face - 128, 128 * face)
            after = slice(128 * face, 128 * face + 128)
            left = [hal[2, c, :, mine] if face == 0 else yt[c, x, 16:32, before] for c in range(10)]
            right = [hal[3, c, :, mine] if face == 2 else yt[c, x, 0:16, after] for c in range(10)]
            out, _, _ = common(left, right, 1)
            for c in range(10):
                h = out[c].astype(BF16)
                if face < 2:
                    hy[c, x, 0:16, after] = h
                if face > 0:
                    hy[c, x, 16:32, before] = h


def faces_z(zt, hz):
    edge = iota((16, 128), 1) == 0
    for t in range(2):
        lanes = slice(128 * t, 128 * t + 128)
        for x in range(2):
            left = [pltpu.roll(zt[c, x, 16:32, lanes], 1, 1) for c in range(10)]
            right = [zt[c, x, 0:16, lanes] for c in range(10)]
            out, fl, fr = common(left, right, 2)
            for c in range(10):
                hz[c, x, 0:16, lanes] = jnp.where(edge, fr[c], out[c]).astype(BF16)
                hz[c, x, 16:32, lanes] = pltpu.roll(jnp.where(edge, fl[c], out[c]), 127, 1).astype(BF16)


def point_fluxes(now, vol):
    @pl.loop(0, 8, unroll=2)
    def _(i):
        x, q = i // 4, pl.multiple_of((i % 4) * 16, 16)
        for t in range(2):
            lanes = slice(128 * t, 128 * t + 128)
            w = [now[c, x, pl.ds(q, 16), lanes] for c in range(10)]
            u, du = w[:5], w[5:]
            r, v, vv, p = primitive(u)
            dv, dp = tangent(du, r, v, vv)
            for d in range(3):
                f, df = flux(u, du, v, p, dv, dp, d)
                for c in range(10):
                    vol[c, x, pl.ds(64 * d + q, 16), lanes] = (f + df)[c].astype(BF16)


def lift_x(hx, c, x, a, scale):
    return float(-scale * LIFT_HI[a]) * hx[c, x + 1] + float(scale * LIFT_LO[a]) * hx[c, x]


def blocks_out(src, dst, sem, g, x):
    return [
        pltpu.make_async_copy(src.at[g, pl.ds(5 * f, 5), x], dst.at[f, :, g, x], sem.at[g, x, f]) for f in range(2)
    ]


def first_section_kernel(field, req, resp, trow, tcol, main_t, trace_t, *refs):
    halo, info, (now_out, mid_out, resp_out), scratch = refs[0:4], refs[4:8], refs[8:11], refs[11:]
    nows, mids, got, lhs, xt, yt, zt, hal, hx, hy, hz, vol, asked, picks, donors, buf, sem, nsem, msem = scratch
    g = pl.program_id(0)
    now, mid = nows.at[g], mids.at[g]

    @pl.when(g == 0)
    def _():
        start_field(field, buf, sem)
        got[...] = resp[...].T
        load_asked(req, asked)

    set_fringe(field, buf, sem, got, trow, tcol, 0, g, lhs, now)
    for x in range(2):
        for copy in blocks_out(nows, now_out, nsem, g, x):
            copy.start()
    all_traces(now, trace_t, xt, yt, zt)
    mend_halos(halo, info, got, 0, g, xt, yt, hal)
    faces_xy(xt, yt, hal, hx, hy)
    faces_z(zt, hz)
    point_fluxes(now, vol)
    for x in range(2):
        columns = pl.ds(pl.multiple_of(512 * g + 256 * x, 256), 256)
        for c in range(10):
            res = dot(main_t[...], jnp.concatenate([vol[c, x], hz[c, x], hy[c, x]], axis=0))
            for a in range(4):
                rows = slice(16 * a, 16 * a + 16)
                new = now[c, x, rows] + (res[rows] + lift_x(hx, c, x, a, DT))
                mid[c, x, rows] = new
                donors[64 * c + 16 * a : 64 * c + 16 * a + 16, columns] = new.astype(BF16)
        for copy in blocks_out(mids, mid_out, msem, g, x):
            copy.start()

    @pl.when(g == 1)
    def _():
        picks[...] = pick(asked, 1, donors)
        resp_out[...] = answer(asked, 1, picks)
        for h in range(2):
            for x in range(2):
                for copy in blocks_out(nows, now_out, nsem, h, x) + blocks_out(mids, mid_out, msem, h, x):
                    copy.wait()


def inner_kernel(field, resp, trow, tcol, main_t, trace_t, partial_out, xt_out, yt_out, *scratch):
    now, got, lhs, zt, hz, vol, buf, sem = scratch
    g = pl.program_id(0)

    @pl.when(g == 0)
    def _():
        start_field(field, buf, sem)
        got[...] = resp[...].T

    set_fringe(field, buf, sem, got, trow, tcol, 1, g, lhs, now)
    all_traces(now, trace_t, xt_out.at[g], yt_out.at[g], zt)
    faces_z(zt, hz)
    point_fluxes(now, vol)
    for x in range(2):
        for c in range(10):
            res = dot(main_t[...], jnp.concatenate([vol[c, x], hz[c, x]], axis=0))
            partial_out[c // 5, c % 5, g, x] = 0.5 * now[c, x] + res


def outer_kernel(part, first, xt, yt, resp, lift_y, *refs):
    halo, info, result, (got, hal, hx, hy) = refs[0:4], refs[4:8], refs[8], refs[9:]
    g = pl.program_id(0)

    @pl.when(g == 0)
    def _():
        got[...] = resp[...].T

    mend_halos(halo, info, got, 1, g, xt.at[g], yt.at[g], hal)
    faces_xy(xt.at[g], yt.at[g], hal, hx, hy)
    for x in range(2):
        for c in range(10):
            res = dot(lift_y[...], hy[c, x])
            for a in range(4):
                rows = slice(16 * a, 16 * a + 16)
                add = res[rows] + lift_x(hx, c, x, a, 0.5 * DT)
                base = part[c // 5, c % 5, g, x, rows] + 0.5 * first[c // 5, c % 5, g, x, rows]
                result[c // 5, c % 5, 0, x, rows] = base + add


FIELD = (2, 5, 2, 2, 64, 256)


def field_spec():
    return pl.BlockSpec((2, 5, 1, 2, 64, 256), lambda g: (0, 0, g, 0, 0, 0))


HERE = pl.BlockSpec(memory_space=pltpu.VMEM)
AWAY = pl.BlockSpec(memory_space=pl.ANY)


def blocks():
    return [pltpu.VMEM((4, 2, 5, 64, 256), F32), pltpu.SemaphoreType.DMA((4,))]


def shape(*dims):
    return jax.ShapeDtypeStruct(dims, F32)


def params(mb):
    return pltpu.CompilerParams(dimension_semantics=("arbitrary",), vmem_limit_bytes=mb * 2**20)


def shift(x, axis, up):
    n = lax.axis_size(axis)
    pairs = [(i, i + 1) if up else (i + 1, i) for i in range(n - 1)]
    return lax.ppermute(x, axis, pairs)


def to_neighbours(traces):
    xlo, xhi, ylo, yhi = traces
    y = [shift(yhi, "tower", True), shift(ylo, "tower", False)]
    return y + [shift(xhi, "rotor", True), shift(xlo, "rotor", False)]


def exchange(x):
    return lax.all_to_all(x, AXES, split_axis=0, concat_axis=0, tiled=True)


def estimate(us):
    return pl.CostEstimate(flops=int(us * 10**9), bytes_accessed=10**5, transcendentals=0)


def vmem(*dims, dtype=F32):
    return pltpu.VMEM(dims, dtype)


def far(x):
    return pltpu.with_memory_space_constraint(x, pltpu.HBM)


def table(scale, columns):
    return jnp.asarray((scale * MAIN[:, columns]).astype(np.float32), BF16)


def trace_call(sec, field, trow, tcol):
    comps = 10 + (sec == 0)
    return pl.pallas_call(
        partial(trace_kernel, sec),
        in_specs=[AWAY, HERE, HERE],
        out_specs=[HERE] * 4,
        out_shape=[pltpu.VMEM((2, comps, 16, 256), F32)] * 4,
        scratch_shapes=blocks(),
        compiler_params=pltpu.CompilerParams(vmem_limit_bytes=16 * 2**20),
        cost_estimate=estimate(2),
        name="traces",
    )(far(field), trow, tcol)


def first_section(field, req, resp, trow, tcol, halos):
    return pl.pallas_call(
        first_section_kernel,
        grid=(2,),
        in_specs=[AWAY] + [HERE] * 14,
        out_specs=[AWAY, AWAY, HERE],
        out_shape=[pltpu.HBM(FIELD, F32), pltpu.HBM(FIELD, F32), shape(128, 128)],
        scratch_shapes=[
            vmem(2, 10, 2, 64, 256),
            vmem(2, 10, 2, 64, 256),
            vmem(128, 128),
            vmem(640, 256, dtype=BF16),
            vmem(10, 2, 32, 256),
            vmem(10, 2, 32, 256),
            vmem(10, 2, 32, 256),
            vmem(4, 10, 16, 256),
            vmem(10, 3, 16, 256),
            vmem(10, 2, 32, 256, dtype=BF16),
            vmem(10, 2, 32, 256, dtype=BF16),
            vmem(10, 2, 192, 256, dtype=BF16),
            vmem(384, 128),
            vmem(640, 256),
            vmem(640, 1024, dtype=BF16),
            *blocks(),
            pltpu.SemaphoreType.DMA((2, 2, 2)),
            pltpu.SemaphoreType.DMA((2, 2, 2)),
        ],
        compiler_params=params(28),
        cost_estimate=estimate(10),
        name="first_section",
    )(far(field), req, resp, trow, tcol, table(-DT, slice(0, 256)), jnp.asarray(TRACE), *halos, *halos)


def inner(field, resp, trow, tcol):
    return pl.pallas_call(
        inner_kernel,
        grid=(2,),
        in_specs=[AWAY] + [HERE] * 5,
        out_specs=[HERE] * 3,
        out_shape=[shape(*FIELD), shape(2, 10, 2, 32, 256), shape(2, 10, 2, 32, 256)],
        scratch_shapes=[
            vmem(10, 2, 64, 256),
            vmem(128, 128),
            vmem(640, 256, dtype=BF16),
            vmem(10, 2, 32, 256),
            vmem(10, 2, 32, 256, dtype=BF16),
            vmem(10, 2, 192, 256, dtype=BF16),
            *blocks(),
        ],
        compiler_params=params(24),
        cost_estimate=estimate(100),
        name="inner",
    )(far(field), resp, trow, tcol, table(-0.5 * DT, slice(0, 224)), jnp.asarray(TRACE))


def outer(part, first, xt, yt, resp, halos, infos):
    return pl.pallas_call(
        outer_kernel,
        grid=(2,),
        in_specs=[HERE] * 14,
        out_specs=field_spec(),
        out_shape=shape(*FIELD),
        scratch_shapes=[
            vmem(128, 128),
            vmem(4, 10, 16, 256),
            vmem(10, 3, 16, 256),
            vmem(10, 2, 32, 256, dtype=BF16),
        ],
        compiler_params=params(24),
        cost_estimate=estimate(10),
        name="outer",
    )(part, first, xt, yt, resp, table(-0.5 * DT, slice(224, 256)), *halos, *infos)


def on_device(field, owner, donor, target, weight):
    req, trow, tcol = pl.pallas_call(
        request_kernel,
        out_shape=[shape(512, 128), shape(8, 256), shape(256, 128)],
        compiler_params=pltpu.CompilerParams(vmem_limit_bytes=16 * 2**20),
        name="request",
    )(
        far(owner.reshape(2, DEV)),
        far(donor.reshape(2, DEV)),
        far(target.reshape(2, DEV)),
        far(jnp.swapaxes(weight[0, 0], 1, 2)),
    )
    req = exchange(req)
    infos = to_neighbours(trace_call(0, field, trow, tcol))
    resp = pl.pallas_call(
        interpolate_kernel,
        in_specs=[AWAY, HERE],
        out_specs=HERE,
        out_shape=shape(128, 128),
        scratch_shapes=[vmem(384, 128), vmem(640, 256), vmem(640, 1024, dtype=BF16)] + blocks(),
        compiler_params=pltpu.CompilerParams(vmem_limit_bytes=16 * 2**20),
        cost_estimate=estimate(100),
        name="interpolate",
    )(far(field), req)
    resp = exchange(resp)
    first, middle, resp = first_section(field, req, resp, trow, tcol, infos)
    resp = exchange(resp)
    halos = to_neighbours(trace_call(1, middle, trow, tcol))
    part, xt, yt = inner(middle, resp, trow, tcol)
    return outer(part, first, xt, yt, resp, halos, infos)


def solution(mesh):
    placed = (
        P(None, None, None, "rotor", None, "tower"),
        P("rotor", "tower", None, None, None),
        P("rotor", "tower", None, None),
        P("rotor", "tower", None, None),
        P("rotor", "tower", None, None, None),
    )
    return jax.shard_map(
        on_device,
        mesh=mesh,
        in_specs=placed,
        out_specs=P(None, None, None, "rotor", None, "tower"),
        check_vma=False,
    )
```
